512 devices in a mesh: dp: 64 (over x, y, core), tensor: 8 (over z).
Axes of the slice: x: 4, y: 8, z: 8, core: 2. Of those that a mesh axis runs over, the one named last changes fastest.
Arguments:
- features: bfloat16 [8192, 4096], P('dp', 'tensor'), may hold values from -6 to 6
- out_grad: bfloat16 [8192, 14336], P('dp', 'tensor'), may hold values from -0.0625 to 0.0625
- weight: bfloat16 [4096, 14336], P('dp', 'tensor'), may hold values from -4 to 4
- basis: bfloat16 [4096, 128], replicated, may hold values from -0.09375 to 0.09375
- moment_one: float32 [8, 1792, 128], P('tensor', 'dp'), may hold values from -3 to 3
- moment_two: float32 [8, 1792, 128], P('tensor', 'dp'), may hold values from 0.05 to 1
Outputs:
- feature_grad: bfloat16 [8192, 4096], P('dp', 'tensor')
- new_moment_one: float32 [8, 1792, 128], P('tensor', 'dp')
- new_moment_two: float32 [8, 1792, 128], P('tensor', 'dp')
- direction: float32 [8, 1792, 4096], P('tensor', 'dp')
The draws below stay inside these ranges and needn't reach their ends.
All inputs are finite; a program needn't handle non-finite values.
Results may differ from the reference program's by a relative error of at most 0.017.
Values may be sent and summed in bfloat16 or wider, within the bound.
No kernel may reach another device: no remote copies, remote signals or barrier semaphores. Data moves between devices by JAX's collectives and lax.ppermute only.
A program may use at most 128 MiB of HBM per device.

```python
import math
import jax
import jax.numpy as jnp
from jax import lax

D = 4096
FF = 14336
R = 128
TOKENS = 8192
FF_T = 1792
N_TENSOR = 8


def steps_of(key, extent, shards, smallest, largest):
    factor_of = 1.0
    for axis_at, blocks in shards:
        heights = jax.random.uniform(jax.random.fold_in(jax.random.fold_in(key, 6), axis_at), (blocks,), jnp.float32, smallest / len(shards), largest / len(shards))
        factor_of = factor_of * jnp.repeat(jnp.exp(heights), extent[axis_at] // blocks).reshape((-1,) + (1,) * (len(extent) - 1 - axis_at))
    return factor_of


def gaussian(key, dims, deviation, limit, shards=(), dtype=jnp.bfloat16):
    entries = jax.random.normal(key, dims, jnp.float32) * deviation
    if len(shards) > 0:
        entries = steps_of(key, dims, shards, -0.22, 0.18) * entries
    return jnp.clip(entries, min=-limit, max=limit).astype(dtype)


def setup_inputs(seed: int = 0) -> dict:
    key_of = jax.random.split(jax.random.key(seed), 7)
    return {
        "features": gaussian(key_of[0], (TOKENS, D), 1.0, 6.0, ((0, 64), (1, 8))),
        "out_grad": gaussian(key_of[1], (TOKENS, FF), (TOKENS ** -0.5), 0.0625, ((0, 64), (1, 8))),
        "weight": gaussian(key_of[2], (D, FF), (FF / TOKENS) ** -0.5, 4.0, ((0, 64), (1, 8))),
        "basis": gaussian(key_of[3], (D, R), D ** -0.5, 0.09375),
        "moment_one": gaussian(key_of[4], (N_TENSOR, FF_T, R), 0.5, 3.0, ((0, 8), (1, 64)), jnp.float32),
        "moment_two": jnp.clip(jnp.exp(math.log(1.0) - 2.9957323 * jax.random.uniform(key_of[5], (N_TENSOR, FF_T, R), jnp.float32) ** steps_of(key_of[5], (N_TENSOR, FF_T, R), ((0, 8), (1, 64)), -0.2, 0.2)), 0.05, 1.0),
    }


beta_one = 0.9
beta_two = 0.95
bias_one = 1.0 - 0.9 ** 20
bias_two = 1.0 - 0.95 ** 20
adam_epsilon = 1e-08

def reference(features, out_grad, weight, basis, moment_one, moment_two):
    block_width = FF // N_TENSOR
    total = jnp.zeros((features.shape[0], D), jnp.float32)
    for block in range(N_TENSOR):
        grad_block = out_grad[:, block * block_width:(block + 1) * block_width]
        weight_block = weight[:, block * block_width:(block + 1) * block_width]
        part = jnp.dot(grad_block, weight_block.T, preferred_element_type=jnp.float32)
        total = total + lax.optimization_barrier(part.astype(jnp.bfloat16)).astype(jnp.float32)
    feature_grad = total.astype(jnp.bfloat16)
    coords = jnp.dot(features, basis, preferred_element_type=jnp.float32).astype(jnp.bfloat16)
    projected = jnp.dot(out_grad.T, coords, preferred_element_type=jnp.float32)
    projected = projected.reshape(N_TENSOR, block_width, R)
    new_one = beta_one * moment_one + (1.0 - beta_one) * projected
    new_two = beta_two * moment_two + (1.0 - beta_two) * projected * projected
    step_dir = (new_one / bias_one / (jnp.sqrt(new_two / bias_two) + adam_epsilon)).astype(jnp.bfloat16)
    direction = jnp.dot(step_dir.reshape(FF, R), basis.T, preferred_element_type=jnp.float32)
    return (feature_grad, new_one, new_two, direction.reshape(N_TENSOR, block_width, D))
```

```python
import jax
import jax.numpy as jnp
from jax import lax
from jax.sharding import PartitionSpec as P

beta_one = 0.9
beta_two = 0.95
bias_one = 1.0 - 0.9**20
bias_two = 1.0 - 0.95**20
adam_epsilon = 1e-08

NX, NY, NC, NZ = 4, 8, 2, 8


def dp_of(x, y, c):
    return (x * NY + y) * NC + c


ALONG_X = [[dp_of(x, y, c) for x in range(NX)] for y in range(NY) for c in range(NC)]
ALONG_YC = [[dp_of(x, y, c) for y in range(NY) for c in range(NC)] for x in range(NX)]

HOME = [
    (dp_of(x, y, c) * NZ + z, dp_of(z // 2, y, c) * NZ + 2 * x + z % 2)
    for x in range(NX)
    for y in range(NY)
    for c in range(NC)
    for z in range(NZ)
]


def body(features, out_grad, weight, basis, moment_one, moment_two):
    tokens, hidden = out_grad.shape
    part_width = features.shape[1]
    rank = basis.shape[1]

    rows = lax.all_gather(weight, "dp", axis=0, tiled=True, axis_index_groups=ALONG_YC)

    basis_part = lax.dynamic_slice_in_dim(
        basis, lax.axis_index("tensor") * part_width, part_width, 0
    )
    local_coords = jnp.dot(features, basis_part, preferred_element_type=jnp.float32)
    all_coords = lax.all_to_all(
        jnp.broadcast_to(local_coords.astype(jnp.bfloat16), (NZ, tokens, rank)), "tensor", 0, 0
    )
    coords = jnp.sum(all_coords.astype(jnp.float32), axis=0).astype(jnp.bfloat16)

    joined = jnp.concatenate([out_grad, coords], axis=1)
    joined = lax.all_to_all(
        jnp.broadcast_to(joined, (NX,) + joined.shape), "dp", 0, 0, axis_index_groups=ALONG_X
    ).reshape(NX * tokens, hidden + rank)
    grads = joined[:, :hidden]
    coords = joined[:, hidden:]

    partial_proj = jnp.einsum("tf,tr->fr", grads, coords, preferred_element_type=jnp.float32)
    own = hidden // NX
    x = lax.axis_index("dp") // (NY * NC)
    partial_proj = lax.dynamic_slice_in_dim(partial_proj, x * own, own, 0)
    partial_proj = lax.all_to_all(
        partial_proj.reshape(NY * NC, own // (NY * NC), rank),
        "dp",
        0,
        0,
        axis_index_groups=ALONG_YC,
    )
    projected = jnp.sum(partial_proj, axis=0)

    first = moment_one[0]
    second = moment_two[0]
    new_one = beta_one * first + (1.0 - beta_one) * projected
    new_two = beta_two * second + (1.0 - beta_two) * projected * projected
    step_dir = (new_one / bias_one / (jnp.sqrt(new_two / bias_two) + adam_epsilon)).astype(
        jnp.bfloat16
    )
    direction = jnp.einsum("cr,dr->cd", step_dir, basis, preferred_element_type=jnp.float32)

    partial_value = jnp.einsum(
        "xtf,hdf->xhtd",
        grads.reshape(NX, tokens, hidden),
        rows.reshape(2, part_width, hidden),
        preferred_element_type=jnp.float32,
    ).astype(jnp.bfloat16)
    pieces = lax.all_to_all(
        partial_value.reshape(NZ, tokens, part_width), "tensor", 0, 0
    )
    summed = jnp.sum(pieces.astype(jnp.float32), axis=0).astype(jnp.bfloat16)
    feature_grad = lax.ppermute(summed, ("dp", "tensor"), HOME)
    return (feature_grad, new_one[None], new_two[None], direction[None])


def solution(mesh):
    in_specs = (
        P("dp", "tensor"),
        P("dp", "tensor"),
        P("dp", "tensor"),
        P(),
        P("tensor", "dp", None),
        P("tensor", "dp", None),
    )
    out_specs = (
        P("dp", "tensor"),
        P("tensor", "dp", None),
        P("tensor", "dp", None),
        P("tensor", "dp", None),
    )
    return jax.shard_map(body, mesh=mesh, in_specs=in_specs, out_specs=out_specs, check_vma=False)
```

```python
import jax
import jax.numpy as jnp
from jax import lax
from jax.experimental import pallas as pl
from jax.experimental.pallas import tpu as pltpu
from jax.sharding import PartitionSpec as P

beta_one = 0.9
beta_two = 0.95
bias_one = 1.0 - 0.9**20
bias_two = 1.0 - 0.95**20
adam_epsilon = 1e-08

NX, NY, NC, NZ = 4, 8, 2, 8


def dp_of(x, y, c):
    return (x * NY + y) * NC + c


CHIPS = [(x, y, c) for x in range(NX) for y in range(NY) for c in range(NC)]
ALONG_X = [[dp_of(x, y, c) for x in range(NX)] for y in range(NY) for c in range(NC)]
ALONG_YC = [[dp_of(x, y, c) for y in range(NY) for c in range(NC)] for x in range(NX)]
SAME_PARITY = [
    [dp_of(x, p + 2 * j, c) for j in range(NY // 2)]
    for x in range(NX)
    for p in range(2)
    for c in range(NC)
]
TO_NEIGHBOUR = [(dp_of(x, y, c), dp_of(x, (y + 1 - 2 * c) % NY, c)) for x, y, c in CHIPS]
OTHER_CORE = [(dp_of(x, y, c), dp_of(x, y, 1 - c)) for x, y, c in CHIPS]

HOME = [
    (dp_of(x, y, c) * NZ + 2 * q + h, dp_of((x + q) % NX, y, c) * NZ + 2 * x + h)
    for x, y, c in CHIPS
    for q in range(NX)
    for h in range(2)
]

FINISH_FLOPS = int(4e9)
VMEM_BYTES = 24 * 1024 * 1024
TILE_VMEM_BYTES = 62 * 1024 * 1024


def whole(count):
    return [pl.BlockSpec(memory_space=pltpu.VMEM)] * count


def in_hbm(count):
    return [pl.BlockSpec(memory_space=pltpu.HBM)] * count


def spread_kernel(grads, out_ref, sems):
    copies = [pltpu.make_async_copy(grads, out_ref.at[x], sems.at[x]) for x in range(NX)]
    for copy in copies:
        copy.start()
    for copy in copies:
        copy.wait()


def spread(grads):
    return pl.pallas_call(
        spread_kernel,
        out_shape=jax.ShapeDtypeStruct((NX,) + grads.shape, grads.dtype),
        in_specs=whole(1),
        out_specs=in_hbm(1)[0],
        scratch_shapes=[pltpu.SemaphoreType.DMA((NX,))],
    )(grads)


def products(left, right, x, out_ref, buffer, sems):
    tokens = out_ref.shape[1]
    half = right.shape[0] // 2
    copies = []
    for h in range(2):
        product = lax.dot_general(
            left[...],
            right[h * half : (h + 1) * half, :],
            (((1,), (1,)), ((), ())),
            preferred_element_type=jnp.float32,
        ).astype(jnp.bfloat16)
        for block in range(NX):
            k = 2 * block + h
            buffer[k, :, :half] = product[block * tokens : (block + 1) * tokens]
            piece = 2 * lax.rem(block - x + NX, NX) + h
            copies.append(
                pltpu.make_async_copy(buffer.at[k], out_ref.at[piece], sems.at[k])
            )
            copies[-1].start()
    return copies


def place(right, height, j, core, mine, other):
    right[pl.ds(pl.multiple_of((NC * j + core) * height, height), height), :] = mine
    right[pl.ds(pl.multiple_of((NC * j + 1 - core) * height, height), height), :] = other


def first_kernel(
    where_ref, left, same, same_other, features, basis, out_ref, near_ref, right, part, buffer,
    sems, near_sems, sem
):
    x, core, z = where_ref[0], where_ref[1], where_ref[2]
    height, width = same.shape[1], features.shape[1]
    start = pl.multiple_of(z * width, width)
    copy = pltpu.make_async_copy(basis.at[pl.ds(start, width), :], part, sem)
    copy.start()
    copies = [
        pltpu.make_async_copy(
            rows.at[pl.ds(NY // 4 * core, NY // 4)], near_ref.at[k], near_sems.at[k]
        )
        for k, rows in enumerate((same, same_other))
    ]
    for near in copies:
        near.start()
    for j in range(NY // 2):
        place(right, height, j, core, same[j], same_other[j])
    copy.wait()
    coords = jnp.dot(features[...], part[...], preferred_element_type=jnp.float32).astype(
        jnp.bfloat16
    )
    for k in range(NZ):
        buffer[k, :, right.shape[0] // 2 :] = coords
    copies += products(left, right, x, out_ref, buffer, sems)
    for piece in copies:
        piece.wait()


def second_kernel(where_ref, left, near, far, out_ref, right, buffer, sems):
    x, core = where_ref[0], where_ref[1]
    height = near.shape[2]
    for j in range(NY // 4):
        place(right, height, NY // 4 * core + j, core, near[0, j], near[1, j])
        place(right, height, NY // 4 * (1 - core) + j, 1 - core, far[0, j], far[1, j])
    for piece in products(left, right, x, out_ref, buffer, sems):
        piece.wait()


def tile_cost(tokens, hidden, rows):
    return pl.CostEstimate(
        flops=2 * tokens * hidden * rows,
        bytes_accessed=2 * (tokens * hidden + rows * hidden + tokens * rows),
        transcendentals=0,
    )


def first_tiles(where, grads, same, same_other, features, basis):
    tokens, hidden = grads.shape[1:]
    count, height = same.shape[:2]
    width, rank = features.shape[1], basis.shape[1]
    rows = 2 * count * height
    return pl.pallas_call(
        first_kernel,
        out_shape=(
            jax.ShapeDtypeStruct((NZ, tokens, rows // 2 + rank), jnp.bfloat16),
            jax.ShapeDtypeStruct((2, count // 2, height, hidden), jnp.bfloat16),
        ),
        in_specs=[pl.BlockSpec(memory_space=pltpu.SMEM)] + whole(4) + in_hbm(1),
        out_specs=tuple(in_hbm(2)),
        scratch_shapes=[
            pltpu.VMEM((rows, hidden), jnp.bfloat16),
            pltpu.VMEM((width, rank), jnp.bfloat16),
            pltpu.VMEM((NZ, tokens, rows // 2 + rank), jnp.bfloat16),
            pltpu.SemaphoreType.DMA((NZ,)),
            pltpu.SemaphoreType.DMA((2,)),
            pltpu.SemaphoreType.DMA,
        ],
        compiler_params=pltpu.CompilerParams(vmem_limit_bytes=TILE_VMEM_BYTES),
        cost_estimate=tile_cost(NX * tokens, hidden, rows),
    )(where, grads.reshape(NX * tokens, hidden), same, same_other, features, basis)


def second_tiles(where, grads, near, far):
    tokens, hidden = grads.shape[1:]
    rows = (near.size + far.size) // hidden
    return pl.pallas_call(
        second_kernel,
        out_shape=jax.ShapeDtypeStruct((NZ, tokens, rows // 2), jnp.bfloat16),
        in_specs=[pl.BlockSpec(memory_space=pltpu.SMEM)] + whole(3),
        out_specs=in_hbm(1)[0],
        scratch_shapes=[
            pltpu.VMEM((rows, hidden), jnp.bfloat16),
            pltpu.VMEM((NZ, tokens, rows // 2), jnp.bfloat16),
            pltpu.SemaphoreType.DMA((NZ,)),
        ],
        compiler_params=pltpu.CompilerParams(vmem_limit_bytes=TILE_VMEM_BYTES),
        cost_estimate=tile_cost(NX * tokens, hidden, rows),
    )(where, grads.reshape(NX * tokens, hidden), near, far)


def sum_kernel(pieces, summed_ref, coords_ref):
    total = jnp.sum(pieces[...].astype(jnp.float32), axis=0)
    width = summed_ref.shape[1]
    summed_ref[...] = total[:, :width]
    coords_ref[...] = total[:, width:].astype(jnp.bfloat16)


def sum_first(pieces, rank):
    tokens, width = pieces.shape[1:]
    return pl.pallas_call(
        sum_kernel,
        out_shape=(
            jax.ShapeDtypeStruct((tokens, width - rank), jnp.float32),
            jax.ShapeDtypeStruct((tokens, rank), jnp.bfloat16),
        ),
        in_specs=whole(1),
        out_specs=tuple(whole(2)),
        compiler_params=pltpu.CompilerParams(vmem_limit_bytes=VMEM_BYTES),
    )(pieces)


def finish_kernel(where_ref, first, second, out_ref):
    parity = where_ref[3]
    width = first.shape[1] // 2
    for j in range(2):
        for mine, at in ((first, parity), (second, 1 - parity)):
            start = pl.multiple_of((2 * j + at) * width, width)
            out_ref[:, pl.ds(start, width)] = mine[:, j * width : (j + 1) * width]


def finish(where, first, second):
    tokens, width = first.shape
    return pl.pallas_call(
        finish_kernel,
        out_shape=jax.ShapeDtypeStruct((tokens, 2 * width), jnp.bfloat16),
        in_specs=[pl.BlockSpec(memory_space=pltpu.SMEM)] + whole(2),
        out_specs=pl.BlockSpec(memory_space=pltpu.VMEM),
        compiler_params=pltpu.CompilerParams(vmem_limit_bytes=VMEM_BYTES),
        cost_estimate=pl.CostEstimate(flops=FINISH_FLOPS, bytes_accessed=0, transcendentals=0),
    )(where, first, second)


def proj_kernel(where_ref, grads, coords, out_ref, proj):
    proj[...] = lax.dot_general(
        grads[...], coords[...], (((0,), (0,)), ((), ())), preferred_element_type=jnp.float32
    )
    parts, share, _ = out_ref.shape
    at = pl.multiple_of(where_ref[0] * (parts * share), parts * share)
    own = proj[pl.ds(at, parts * share), :]
    for k in range(parts):
        out_ref[k] = own[k * share : (k + 1) * share]


def project(where, grads, coords):
    hidden, rank = grads.shape[2], coords.shape[1]
    return pl.pallas_call(
        proj_kernel,
        out_shape=jax.ShapeDtypeStruct((NY * NC, hidden // (NX * NY * NC), rank), jnp.float32),
        in_specs=[pl.BlockSpec(memory_space=pltpu.SMEM)] + whole(2),
        out_specs=pl.BlockSpec(memory_space=pltpu.VMEM),
        scratch_shapes=[pltpu.VMEM((hidden, rank), jnp.float32)],
        compiler_params=pltpu.CompilerParams(vmem_limit_bytes=VMEM_BYTES),
    )(where, grads.reshape(-1, hidden), coords)


def adam_kernel(parts_ref, basis_ref, one_ref, two_ref, new_one_ref, new_two_ref, direction_ref):
    projected = jnp.sum(parts_ref[...], axis=0)
    new_one = beta_one * one_ref[:, 0, :] + (1.0 - beta_one) * projected
    new_two = beta_two * two_ref[:, 0, :] + (1.0 - beta_two) * projected * projected
    new_one_ref[:, 0, :] = new_one
    new_two_ref[:, 0, :] = new_two
    step_dir = new_one / bias_one / (jnp.sqrt(new_two / bias_two) + adam_epsilon)
    direction_ref[:, 0, :] = lax.dot_general(
        step_dir.astype(jnp.bfloat16),
        basis_ref[...],
        (((1,), (1,)), ((), ())),
        preferred_element_type=jnp.float32,
    )


def adam(parts, basis, one, two):
    rows = one.shape[0]
    return pl.pallas_call(
        adam_kernel,
        out_shape=(
            jax.ShapeDtypeStruct(one.shape, jnp.float32),
            jax.ShapeDtypeStruct(one.shape, jnp.float32),
            jax.ShapeDtypeStruct((rows, 1, basis.shape[0]), jnp.float32),
        ),
        in_specs=whole(4),
        out_specs=tuple(whole(3)),
        compiler_params=pltpu.CompilerParams(vmem_limit_bytes=VMEM_BYTES),
    )(parts, basis, one, two)


def body(features, out_grad, weight, basis, moment_one, moment_two):
    dp = lax.axis_index("dp")
    x, y, core = dp // (NY * NC), (dp // NC) % NY, dp % NC
    where = jnp.stack([x, core, lax.axis_index("tensor"), y % 2])

    grads = lax.all_to_all(spread(out_grad), "dp", 0, 0, axis_index_groups=ALONG_X)
    same = lax.all_gather(weight, "dp", axis=0, axis_index_groups=SAME_PARITY)
    same, grads = lax.optimization_barrier((same, grads))

    same_other = lax.ppermute(same, "dp", OTHER_CORE)
    first, near = first_tiles(where, grads, same, same_other, features, basis)
    first = lax.all_to_all(first, "tensor", 0, 0)

    near = lax.ppermute(near, "dp", TO_NEIGHBOUR)
    far = lax.ppermute(near, "dp", OTHER_CORE)
    second = second_tiles(where, grads, near, far)
    first, second = lax.optimization_barrier((first, second))
    second = lax.all_to_all(second, "tensor", 0, 0)
    first, coords = sum_first(first, basis.shape[1])

    coords = lax.all_gather(coords, "dp", axis=0, tiled=True, axis_index_groups=ALONG_X)
    parts = project(where, grads, coords)
    parts, second = lax.optimization_barrier((parts, second))

    summed = jnp.sum(second.astype(jnp.float32), axis=0)
    summed = jnp.concatenate([first, summed], axis=1).astype(jnp.bfloat16)
    summed = lax.ppermute(summed, ("dp", "tensor"), HOME)
    half = summed.shape[1] // 2
    feature_grad = finish(where, summed[:, :half], summed[:, half:])

    parts = lax.all_to_all(parts, "dp", 0, 0, axis_index_groups=ALONG_YC)
    results = adam(parts, basis, *(jnp.swapaxes(m, 0, 1) for m in (moment_one, moment_two)))
    return (feature_grad, *(jnp.swapaxes(r, 0, 1) for r in results))


def solution(mesh):
    in_specs = (
        P("dp", "tensor"),
        P("dp", "tensor"),
        P("dp", "tensor"),
        P(),
        P("tensor", "dp", None),
        P("tensor", "dp", None),
    )
    out_specs = (
        P("dp", "tensor"),
        P("tensor", "dp", None),
        P("tensor", "dp", None),
        P("tensor", "dp", None),
    )
    return jax.shard_map(body, mesh=mesh, in_specs=in_specs, out_specs=out_specs, check_vma=False)
```

```python
import jax
import jax.numpy as jnp
from jax import lax
from jax.experimental import pallas as pl
from jax.experimental.pallas import tpu as pltpu
from jax.sharding import PartitionSpec as P

beta_one = 0.9
beta_two = 0.95
bias_one = 1.0 - 0.9**20
bias_two = 1.0 - 0.95**20
adam_epsilon = 1e-08

NX, NY, NC, NZ = 4, 8, 2, 8


def dp_of(x, y, c):
    return (x * NY + y) * NC + c


def here():
    dp = lax.axis_index("dp")
    y = lax.rem(lax.div(dp, NC), NY)
    return lax.div(dp, NY * NC), y, lax.rem(dp, NC), lax.axis_index("tensor")


CHIPS = [(x, y, c) for x in range(NX) for y in range(NY) for c in range(NC)]
ALONG_X = [[dp_of(x, y, c) for x in range(NX)] for y in range(NY) for c in range(NC)]
ALONG_Y = [[dp_of(x, y, c) for y in range(NY)] for x in range(NX) for c in range(NC)]
SAME_PARITY = [
    [dp_of(x, p + 2 * j, c) for j in range(NY // 2)]
    for x in range(NX)
    for p in range(2)
    for c in range(NC)
]
TO_NEIGHBOUR = [(dp_of(x, y, c), dp_of(x, (y + 1 - 2 * c) % NY, c)) for x, y, c in CHIPS]
OTHER_CORE = [(dp_of(x, y, c), dp_of(x, y, 1 - c)) for x, y, c in CHIPS]

HOME = [
    (dp_of(x, y, c) * NZ + 2 * q + h, dp_of((x + q) % NX, y, c) * NZ + 2 * x + h)
    for x, y, c in CHIPS
    for q in range(NX)
    for h in range(2)
]

FINISH_FLOPS = int(4e9)
FIRST_FLOPS = int(1e9)
SECOND_FLOPS = int(1e9)
VMEM_BYTES = 24 * 1024 * 1024
FIRST_VMEM = 53_000_000
SECOND_VMEM = 24_000_000


def whole(count):
    return [pl.BlockSpec(memory_space=pltpu.VMEM)] * count


def in_hbm(count):
    return [pl.BlockSpec(memory_space=pltpu.HBM)] * count


def spread_kernel(grads, out_ref, sems):
    copies = [pltpu.make_async_copy(grads, out_ref.at[x], sems.at[x]) for x in range(NX)]
    for copy in copies:
        copy.start()
    for copy in copies:
        copy.wait()


def spread(grads):
    return pl.pallas_call(
        spread_kernel,
        out_shape=jax.ShapeDtypeStruct((NX,) + grads.shape, grads.dtype),
        in_specs=whole(1),
        out_specs=in_hbm(1)[0],
        scratch_shapes=[pltpu.SemaphoreType.DMA((NX,))],
    )(grads)


def products(left, right, x, out_ref, buffer, sems):
    tokens = out_ref.shape[1]
    half = right.shape[0] // 2
    copies = []
    for h in range(2):
        product = lax.dot_general(
            left[...],
            right[h * half : (h + 1) * half, :],
            (((1,), (1,)), ((), ())),
            preferred_element_type=jnp.float32,
        ).astype(jnp.bfloat16)
        for block in range(NX):
            k = 2 * block + h
            buffer[k, :, :half] = product[block * tokens : (block + 1) * tokens]
            piece = 2 * lax.rem(block - x + NX, NX) + h
            copies.append(
                pltpu.make_async_copy(buffer.at[k], out_ref.at[piece], sems.at[k])
            )
            copies[-1].start()
    return copies


def place(right, height, j, core, mine, other):
    right[pl.ds(pl.multiple_of((NC * j + core) * height, height), height), :] = mine
    right[pl.ds(pl.multiple_of((NC * j + 1 - core) * height, height), height), :] = other


def first_kernel(
    left, same, same_other, features, basis, out_ref, near_ref, right, part, buffer,
    sems, near_sems, sem
):
    x, _, core, z = here()
    height, width = same.shape[1], features.shape[1]
    start = pl.multiple_of(z * width, width)
    copy = pltpu.make_async_copy(basis.at[pl.ds(start, width), :], part, sem)
    copy.start()
    copies = [
        pltpu.make_async_copy(
            rows.at[pl.ds(NY // 4 * core, NY // 4)], near_ref.at[k], near_sems.at[k]
        )
        for k, rows in enumerate((same, same_other))
    ]
    for near in copies:
        near.start()
    for j in range(NY // 2):
        place(right, height, j, core, same[j], same_other[j])
    copy.wait()
    coords = jnp.dot(features[...], part[...], preferred_element_type=jnp.float32).astype(
        jnp.bfloat16
    )
    for k in range(NZ):
        buffer[k, :, right.shape[0] // 2 :] = coords
    copies += products(left, right, x, out_ref, buffer, sems)
    for piece in copies:
        piece.wait()


def second_kernel(left, near, far, out_ref, right, buffer, sems):
    x, _, core, _ = here()
    height = near.shape[2]
    for j in range(NY // 4):
        place(right, height, NY // 4 * core + j, core, near[0, j], near[1, j])
        place(right, height, NY // 4 * (1 - core) + j, 1 - core, far[0, j], far[1, j])
    for piece in products(left, right, x, out_ref, buffer, sems):
        piece.wait()


def first_tiles(grads, same, same_other, features, basis):
    tokens, hidden = grads.shape[1:]
    count, height = same.shape[:2]
    width, rank = features.shape[1], basis.shape[1]
    rows = 2 * count * height
    return pl.pallas_call(
        first_kernel,
        out_shape=(
            jax.ShapeDtypeStruct((NZ, tokens, rows // 2 + rank), jnp.bfloat16),
            jax.ShapeDtypeStruct((2, count // 2, height, hidden), jnp.bfloat16),
        ),
        in_specs=whole(4) + in_hbm(1),
        out_specs=tuple(in_hbm(2)),
        scratch_shapes=[
            pltpu.VMEM((rows, hidden), jnp.bfloat16),
            pltpu.VMEM((width, rank), jnp.bfloat16),
            pltpu.VMEM((NZ, tokens, rows // 2 + rank), jnp.bfloat16),
            pltpu.SemaphoreType.DMA((NZ,)),
            pltpu.SemaphoreType.DMA((2,)),
            pltpu.SemaphoreType.DMA,
        ],
        compiler_params=pltpu.CompilerParams(vmem_limit_bytes=FIRST_VMEM),
        cost_estimate=pl.CostEstimate(flops=FIRST_FLOPS, bytes_accessed=0, transcendentals=0),
    )(grads.reshape(NX * tokens, hidden), same, same_other, features, basis)


def second_tiles(grads, near, far):
    tokens, hidden = grads.shape[1:]
    rows = (near.size + far.size) // hidden
    return pl.pallas_call(
        second_kernel,
        out_shape=jax.ShapeDtypeStruct((NZ, tokens, rows // 2), jnp.bfloat16),
        in_specs=whole(3),
        out_specs=in_hbm(1)[0],
        scratch_shapes=[
            pltpu.VMEM((rows, hidden), jnp.bfloat16),
            pltpu.VMEM((NZ, tokens, rows // 2), jnp.bfloat16),
            pltpu.SemaphoreType.DMA((NZ,)),
        ],
        compiler_params=pltpu.CompilerParams(vmem_limit_bytes=SECOND_VMEM),
        cost_estimate=pl.CostEstimate(flops=SECOND_FLOPS, bytes_accessed=0, transcendentals=0),
    )(grads.reshape(NX * tokens, hidden), near, far)


def sum_kernel(pieces, summed_ref, coords_ref):
    total = jnp.sum(pieces[...].astype(jnp.float32), axis=0)
    width = summed_ref.shape[1]
    summed_ref[...] = total[:, :width]
    coords_ref[...] = total[:, width:].astype(jnp.bfloat16)


def sum_first(pieces, rank):
    tokens, width = pieces.shape[1:]
    return pl.pallas_call(
        sum_kernel,
        out_shape=(
            jax.ShapeDtypeStruct((tokens, width - rank), jnp.float32),
            jax.ShapeDtypeStruct((tokens, rank), jnp.bfloat16),
        ),
        in_specs=whole(1),
        out_specs=tuple(whole(2)),
        compiler_params=pltpu.CompilerParams(vmem_limit_bytes=VMEM_BYTES),
    )(pieces)


def finish_kernel(first, second, out_ref):
    parity = lax.rem(here()[1], 2)
    width = first.shape[1] // 2
    for j in range(2):
        for mine, at in ((first, parity), (second, 1 - parity)):
            start = pl.multiple_of((2 * j + at) * width, width)
            out_ref[:, pl.ds(start, width)] = mine[:, j * width : (j + 1) * width]


def finish(first, second):
    tokens, width = first.shape
    return pl.pallas_call(
        finish_kernel,
        out_shape=jax.ShapeDtypeStruct((tokens, 2 * width), jnp.bfloat16),
        in_specs=whole(2),
        out_specs=pl.BlockSpec(memory_space=pltpu.VMEM),
        compiler_params=pltpu.CompilerParams(vmem_limit_bytes=VMEM_BYTES),
        cost_estimate=pl.CostEstimate(flops=FINISH_FLOPS, bytes_accessed=0, transcendentals=0),
    )(first, second)


def proj_kernel(grads, coords, mine_ref, other_ref, proj):
    proj[...] = lax.dot_general(
        grads[...], coords[...], (((0,), (0,)), ((), ())), preferred_element_type=jnp.float32
    )
    x, _, core, _ = here()
    parts, share, _ = mine_ref.shape
    rows = parts * NC * share
    own = proj[pl.ds(pl.multiple_of(x * rows, rows), rows), :]
    first_core = core == 0
    for k in range(parts):
        at = NC * k * share
        zero, one = own[at : at + share], own[at + share : at + NC * share]
        mine_ref[k] = jnp.where(first_core, zero, one)
        other_ref[k] = jnp.where(first_core, one, zero)


def project(grads, coords):
    hidden, rank = grads.shape[2], coords.shape[1]
    part = jax.ShapeDtypeStruct((NY, hidden // (NX * NY * NC), rank), jnp.float32)
    return pl.pallas_call(
        proj_kernel,
        out_shape=(part, part),
        in_specs=whole(2),
        out_specs=tuple(whole(2)),
        scratch_shapes=[pltpu.VMEM((hidden, rank), jnp.float32)],
        compiler_params=pltpu.CompilerParams(vmem_limit_bytes=VMEM_BYTES),
    )(grads.reshape(-1, hidden), coords)


def adam_kernel(parts_ref, basis_ref, one_ref, two_ref, new_one_ref, new_two_ref, direction_ref):
    projected = jnp.sum(parts_ref[...], axis=0)
    new_one = beta_one * one_ref[:, 0, :] + (1.0 - beta_one) * projected
    new_two = beta_two * two_ref[:, 0, :] + (1.0 - beta_two) * projected * projected
    new_one_ref[:, 0, :] = new_one
    new_two_ref[:, 0, :] = new_two
    step_dir = new_one / bias_one / (jnp.sqrt(new_two / bias_two) + adam_epsilon)
    direction_ref[:, 0, :] = lax.dot_general(
        step_dir.astype(jnp.bfloat16),
        basis_ref[...],
        (((1,), (1,)), ((), ())),
        preferred_element_type=jnp.float32,
    )


def adam(parts, basis, one, two):
    rows = one.shape[0]
    return pl.pallas_call(
        adam_kernel,
        out_shape=(
            jax.ShapeDtypeStruct(one.shape, jnp.float32),
            jax.ShapeDtypeStruct(one.shape, jnp.float32),
            jax.ShapeDtypeStruct((rows, 1, basis.shape[0]), jnp.float32),
        ),
        in_specs=whole(4),
        out_specs=tuple(whole(3)),
        compiler_params=pltpu.CompilerParams(vmem_limit_bytes=VMEM_BYTES),
    )(parts, basis, one, two)


def body(features, out_grad, weight, basis, moment_one, moment_two):
    grads = lax.all_to_all(spread(out_grad), "dp", 0, 0, axis_index_groups=ALONG_X)
    same = lax.all_gather(weight, "dp", axis=0, axis_index_groups=SAME_PARITY)

    same_other = lax.ppermute(same, "dp", OTHER_CORE)
    first, near = first_tiles(grads, same, same_other, features, basis)
    first = lax.all_to_all(first, "tensor", 0, 0)

    near = lax.ppermute(near, "dp", TO_NEIGHBOUR)
    far = lax.ppermute(near, "dp", OTHER_CORE)
    second = second_tiles(grads, near, far)
    first, second = lax.optimization_barrier((first, second))
    second = lax.all_to_all(second, "tensor", 0, 0)
    first, coords = sum_first(first, basis.shape[1])

    coords = lax.all_gather(coords, "dp", axis=0, tiled=True, axis_index_groups=ALONG_X)
    parts, other = project(grads, coords)
    parts = parts + lax.ppermute(other, "dp", OTHER_CORE)
    parts, second = lax.optimization_barrier((parts, second))

    summed = jnp.sum(second.astype(jnp.float32), axis=0)
    summed = jnp.concatenate([first, summed], axis=1).astype(jnp.bfloat16)
    summed = lax.ppermute(summed, ("dp", "tensor"), HOME)
    half = summed.shape[1] // 2
    feature_grad = finish(summed[:, :half], summed[:, half:])

    parts = lax.all_to_all(parts, "dp", 0, 0, axis_index_groups=ALONG_Y)
    results = adam(parts, basis, *(jnp.swapaxes(m, 0, 1) for m in (moment_one, moment_two)))
    return (feature_grad, *(jnp.swapaxes(r, 0, 1) for r in results))


def solution(mesh):
    in_specs = (
        P("dp", "tensor"),
        P("dp", "tensor"),
        P("dp", "tensor"),
        P(),
        P("tensor", "dp", None),
        P("tensor", "dp", None),
    )
    out_specs = (
        P("dp", "tensor"),
        P("tensor", "dp", None),
        P("tensor", "dp", None),
        P("tensor", "dp", None),
    )
    return jax.shard_map(body, mesh=mesh, in_specs=in_specs, out_specs=out_specs, check_vma=False)
```

```python
import jax
import jax.numpy as jnp
from jax import lax
from jax.experimental import pallas as pl
from jax.experimental.pallas import tpu as pltpu
from jax.sharding import PartitionSpec as P

beta_one = 0.9
beta_two = 0.95
bias_one = 1.0 - 0.9**20
bias_two = 1.0 - 0.95**20
adam_epsilon = 1e-08

NX, NY, NC, NZ = 4, 8, 2, 8


def dp_of(x, y, c):
    return (x * NY + y) * NC + c


def here():
    dp = lax.axis_index("dp")
    y = lax.rem(lax.div(dp, NC), NY)
    return lax.div(dp, NY * NC), y, lax.rem(dp, NC), lax.axis_index("tensor")


CHIPS = [(x, y, c) for x in range(NX) for y in range(NY) for c in range(NC)]
ALONG_X = [[dp_of(x, y, c) for x in range(NX)] for y in range(NY) for c in range(NC)]
ALONG_Y = [[dp_of(x, y, c) for y in range(NY)] for x in range(NX) for c in range(NC)]
SAME_PARITY = [
    [dp_of(x, p + 2 * j, c) for j in range(NY // 2)]
    for x in range(NX)
    for p in range(2)
    for c in range(NC)
]
TO_NEIGHBOUR = [(dp_of(x, y, c), dp_of(x, (y + 1 - 2 * c) % NY, c)) for x, y, c in CHIPS]
OTHER_CORE = [(dp_of(x, y, c), dp_of(x, y, 1 - c)) for x, y, c in CHIPS]

HOME = [
    (dp_of(x, y, c) * NZ + 2 * q + h, dp_of((x + q) % NX, y, c) * NZ + 2 * x + h)
    for x, y, c in CHIPS
    for q in range(NX)
    for h in range(2)
]

FINISH_FLOPS = int(4e9)
FIRST_FLOPS = int(1e9)
SECOND_FLOPS = int(1e9)
NEAR_FLOPS = int(1e9)
NEAR_VMEM = 24_000_000
VMEM_BYTES = 24 * 1024 * 1024
FIRST_VMEM = 53_000_000
SECOND_VMEM = 53_000_000


def whole(count):
    return [pl.BlockSpec(memory_space=pltpu.VMEM)] * count


def in_hbm(count):
    return [pl.BlockSpec(memory_space=pltpu.HBM)] * count


def spread_kernel(grads, out_ref, sems):
    copies = [pltpu.make_async_copy(grads, out_ref.at[x], sems.at[x]) for x in range(NX)]
    for copy in copies:
        copy.start()
    for copy in copies:
        copy.wait()


def spread(grads):
    return pl.pallas_call(
        spread_kernel,
        out_shape=jax.ShapeDtypeStruct((NX,) + grads.shape, grads.dtype),
        in_specs=whole(1),
        out_specs=in_hbm(1)[0],
        scratch_shapes=[pltpu.SemaphoreType.DMA((NX,))],
    )(grads)


FOLD = 4


def folded(block):
    step = block.shape[0] // FOLD
    return jnp.concatenate([block[k * step : (k + 1) * step] for k in range(FOLD)], axis=1)


def unfolded(block):
    step = block.shape[1] // FOLD
    return jnp.concatenate([block[:, k * step : (k + 1) * step] for k in range(FOLD)], axis=0)


def times(left, rows):
    return lax.dot_general(
        left[...], rows, (((1,), (1,)), ((), ())), preferred_element_type=jnp.float32
    ).astype(jnp.bfloat16)


def other_rows(same_other, k):
    height = same_other.shape[0] // (NY // 2)
    return jnp.concatenate(
        [same_other[(2 * h + k) * height : (2 * h + k + 1) * height, :] for h in range(2)], axis=0
    )


def fill(buffer, at, tokens, product):
    width = product.shape[1] // 2
    for block in range(NX):
        for h in range(2):
            part = product[block * tokens : (block + 1) * tokens, h * width : (h + 1) * width]
            if at is None:
                buffer[2 * block + h, tokens:, :] = folded(part)
            else:
                buffer[2 * block + h, :tokens, at : at + width] = part


def send(buffer, out_ref, x, sems):
    copies = []
    for block in range(NX):
        for h in range(2):
            k = 2 * block + h
            piece = 2 * lax.rem(block - x + NX, NX) + h
            copies.append(pltpu.make_async_copy(buffer.at[k], out_ref.at[piece], sems.at[k]))
            copies[-1].start()
    for copy in copies:
        copy.wait()


def first_kernel(left, same, same_other, features, basis, out_ref, part, buffer, sems, sem):
    x, _, _, z = here()
    tokens, width = features.shape
    rank = basis.shape[1]
    start = pl.multiple_of(z * width, width)
    copy = pltpu.make_async_copy(basis.at[pl.ds(start, width), :], part, sem)
    copy.start()
    fill(buffer, 0, tokens, times(left, same[...]))
    fill(buffer, None, tokens, times(left, other_rows(same_other, 0)))
    copy.wait()
    coords = jnp.dot(features[...], part[...], preferred_element_type=jnp.float32).astype(
        jnp.bfloat16
    )
    for k in range(NZ):
        buffer[k, :tokens, buffer.shape[2] - rank :] = coords
    send(buffer, out_ref, x, sems)


def near_kernel(same, same_other, near_ref):
    _, _, core, _ = here()
    for k, rows in enumerate((same, same_other)):
        for j in range(NY // 4):
            near_ref[k, j] = rows[NY // 4 * core + j]


def rest_kernel(left, same_other, near, far, out_ref, right, buffer, sems):
    x, _, core, _ = here()
    height = near.shape[2]
    tokens = left.shape[0] // NX

    def place(j, c, rows):
        at = pl.multiple_of((NC * j + c) * height, height)
        right[pl.ds(at, height), :] = rows

    for j in range(NY // 4):
        for source, half in ((near, core), (far, 1 - core)):
            place(NY // 4 * half + j, half, source[0, j])
            place(NY // 4 * half + j, 1 - half, source[1, j])
    fill(buffer, None, tokens, times(left, other_rows(same_other, 1)))
    fill(buffer, 0, tokens, times(left, right[...]))
    send(buffer, out_ref, x, sems)


def flat(rows):
    return rows.reshape(-1, rows.shape[-1])


def first_tiles(grads, same, same_other, features, basis):
    tokens, width = features.shape
    rank = basis.shape[1]
    same, same_other = flat(same), flat(same_other)
    shape = (NZ, tokens + tokens // FOLD, same.shape[0] // 2 + rank)
    return pl.pallas_call(
        first_kernel,
        out_shape=jax.ShapeDtypeStruct(shape, jnp.bfloat16),
        in_specs=whole(4) + in_hbm(1),
        out_specs=in_hbm(1)[0],
        scratch_shapes=[
            pltpu.VMEM((width, rank), jnp.bfloat16),
            pltpu.VMEM(shape, jnp.bfloat16),
            pltpu.SemaphoreType.DMA((NZ,)),
            pltpu.SemaphoreType.DMA,
        ],
        compiler_params=pltpu.CompilerParams(vmem_limit_bytes=FIRST_VMEM),
        cost_estimate=pl.CostEstimate(flops=FIRST_FLOPS, bytes_accessed=0, transcendentals=0),
    )(flat(grads), same, same_other, features, basis)


def neighbour_rows(same, same_other):
    count, height, hidden = same.shape
    return pl.pallas_call(
        near_kernel,
        out_shape=jax.ShapeDtypeStruct((2, count // 2, height, hidden), jnp.bfloat16),
        in_specs=whole(2),
        out_specs=whole(1)[0],
        compiler_params=pltpu.CompilerParams(vmem_limit_bytes=NEAR_VMEM),
        cost_estimate=pl.CostEstimate(flops=NEAR_FLOPS, bytes_accessed=0, transcendentals=0),
    )(same, same_other)


def rest_tiles(grads, same_other, near, far):
    tokens, hidden = grads.shape[1:]
    same_other = flat(same_other)
    rows = (near.size + far.size) // hidden
    shape = (NZ, tokens + tokens // FOLD, rows // 2)
    return pl.pallas_call(
        rest_kernel,
        out_shape=jax.ShapeDtypeStruct(shape, jnp.bfloat16),
        in_specs=whole(4),
        out_specs=in_hbm(1)[0],
        scratch_shapes=[
            pltpu.VMEM((rows, hidden), jnp.bfloat16),
            pltpu.VMEM(shape, jnp.bfloat16),
            pltpu.SemaphoreType.DMA((NZ,)),
        ],
        compiler_params=pltpu.CompilerParams(vmem_limit_bytes=SECOND_VMEM),
        cost_estimate=pl.CostEstimate(flops=SECOND_FLOPS, bytes_accessed=0, transcendentals=0),
    )(flat(grads), same_other, near, far)


def sum_kernel(pieces, summed_ref, coords_ref):
    total = jnp.sum(pieces[...].astype(jnp.float32), axis=0)
    tokens, rank = coords_ref.shape
    width = total.shape[1] - rank
    summed_ref[:, :width] = total[:tokens, :width]
    summed_ref[:, width:] = unfolded(total[tokens:])
    coords_ref[...] = total[:tokens, width:].astype(jnp.bfloat16)


def sum_first(pieces, rank):
    tokens = pieces.shape[1] * FOLD // (FOLD + 1)
    width = pieces.shape[2]
    return pl.pallas_call(
        sum_kernel,
        out_shape=(
            jax.ShapeDtypeStruct((tokens, width - rank + width // FOLD), jnp.float32),
            jax.ShapeDtypeStruct((tokens, rank), jnp.bfloat16),
        ),
        in_specs=whole(1),
        out_specs=tuple(whole(2)),
        compiler_params=pltpu.CompilerParams(vmem_limit_bytes=VMEM_BYTES),
    )(pieces)


def join_kernel(first, pieces, out_ref):
    total = jnp.sum(pieces[...].astype(jnp.float32), axis=0)
    tokens, width = first.shape
    out_ref[:, :width] = first[...].astype(jnp.bfloat16)
    rest = unfolded(total[tokens:])
    out_ref[:, width : width + rest.shape[1]] = rest.astype(jnp.bfloat16)
    out_ref[:, width + rest.shape[1] :] = total[:tokens].astype(jnp.bfloat16)


def join(first, pieces):
    tokens, width = first.shape
    columns = width + pieces.shape[2] // FOLD + pieces.shape[2]
    return pl.pallas_call(
        join_kernel,
        out_shape=jax.ShapeDtypeStruct((tokens, columns), jnp.bfloat16),
        in_specs=whole(2),
        out_specs=whole(1)[0],
        compiler_params=pltpu.CompilerParams(vmem_limit_bytes=VMEM_BYTES),
    )(first, pieces)


def finish_kernel(parts, out_ref):
    _, y, core, _ = here()
    parity = lax.rem(y, 2)
    width = out_ref.shape[1] // (NY // 2 * NC)
    for k in range(2):
        mine = parts[:, k * width : (k + 1) * width]
        other = parts[:, (2 + k) * width : (3 + k) * width]
        for odd in range(2):
            for c in range(NC):
                crossed = parts[:, (4 + NC * k + c) * width : (5 + NC * k + c) * width]
                at = ((2 * k + odd) * NC + c) * width
                out_ref[:, at : at + width] = jnp.where(
                    parity == odd, jnp.where(core == c, mine, other), crossed
                )


def finish(parts):
    return pl.pallas_call(
        finish_kernel,
        out_shape=jax.ShapeDtypeStruct(parts.shape, jnp.bfloat16),
        in_specs=whole(1),
        out_specs=pl.BlockSpec(memory_space=pltpu.VMEM),
        compiler_params=pltpu.CompilerParams(vmem_limit_bytes=VMEM_BYTES),
        cost_estimate=pl.CostEstimate(flops=FINISH_FLOPS, bytes_accessed=0, transcendentals=0),
    )(parts)


def proj_kernel(grads, coords, mine_ref, other_ref, proj):
    proj[...] = lax.dot_general(
        grads[...], coords[...], (((0,), (0,)), ((), ())), preferred_element_type=jnp.float32
    )
    x, _, core, _ = here()
    parts, share, _ = mine_ref.shape
    rows = parts * NC * share
    own = proj[pl.ds(pl.multiple_of(x * rows, rows), rows), :]
    first_core = core == 0
    for k in range(parts):
        at = NC * k * share
        zero, one = own[at : at + share], own[at + share : at + NC * share]
        mine_ref[k] = jnp.where(first_core, zero, one)
        other_ref[k] = jnp.where(first_core, one, zero)


def project(grads, coords):
    hidden, rank = grads.shape[2], coords.shape[1]
    part = jax.ShapeDtypeStruct((NY, hidden // (NX * NY * NC), rank), jnp.float32)
    return pl.pallas_call(
        proj_kernel,
        out_shape=(part, part),
        in_specs=whole(2),
        out_specs=tuple(whole(2)),
        scratch_shapes=[pltpu.VMEM((hidden, rank), jnp.float32)],
        compiler_params=pltpu.CompilerParams(vmem_limit_bytes=VMEM_BYTES),
    )(grads.reshape(-1, hidden), coords)


def adam_kernel(parts_ref, basis_ref, one_ref, two_ref, new_one_ref, new_two_ref, direction_ref):
    projected = jnp.sum(parts_ref[...], axis=0)
    new_one = beta_one * one_ref[:, 0, :] + (1.0 - beta_one) * projected
    new_two = beta_two * two_ref[:, 0, :] + (1.0 - beta_two) * projected * projected
    new_one_ref[:, 0, :] = new_one
    new_two_ref[:, 0, :] = new_two
    step_dir = new_one / bias_one / (jnp.sqrt(new_two / bias_two) + adam_epsilon)
    direction_ref[:, 0, :] = lax.dot_general(
        step_dir.astype(jnp.bfloat16),
        basis_ref[...],
        (((1,), (1,)), ((), ())),
        preferred_element_type=jnp.float32,
    )


def adam(parts, basis, one, two):
    rows = one.shape[0]
    return pl.pallas_call(
        adam_kernel,
        out_shape=(
            jax.ShapeDtypeStruct(one.shape, jnp.float32),
            jax.ShapeDtypeStruct(one.shape, jnp.float32),
            jax.ShapeDtypeStruct((rows, 1, basis.shape[0]), jnp.float32),
        ),
        in_specs=whole(4),
        out_specs=tuple(whole(3)),
        compiler_params=pltpu.CompilerParams(vmem_limit_bytes=VMEM_BYTES),
    )(parts, basis, one, two)


def body(features, out_grad, weight, basis, moment_one, moment_two):
    grads = lax.all_to_all(spread(out_grad), "dp", 0, 0, axis_index_groups=ALONG_X)
    same = lax.all_gather(weight, "dp", axis=0, axis_index_groups=SAME_PARITY)

    same_other = lax.ppermute(same, "dp", OTHER_CORE)
    first = first_tiles(grads, same, same_other, features, basis)
    first, same, same_other = lax.optimization_barrier((first, same, same_other))
    first = lax.all_to_all(first, "tensor", 0, 0)

    near = lax.ppermute(neighbour_rows(same, same_other), "dp", TO_NEIGHBOUR)
    far = lax.ppermute(near, "dp", OTHER_CORE)
    second = rest_tiles(grads, same_other, near, far)
    first, second = lax.optimization_barrier((first, second))
    second = lax.all_to_all(second, "tensor", 0, 0)
    first, coords = sum_first(first, basis.shape[1])

    coords = lax.all_gather(coords, "dp", axis=0, tiled=True, axis_index_groups=ALONG_X)
    parts, other = project(grads, coords)
    parts = parts + lax.ppermute(other, "dp", OTHER_CORE)
    parts, second = lax.optimization_barrier((parts, second))

    summed = lax.ppermute(join(first, second), ("dp", "tensor"), HOME)
    feature_grad = finish(summed)

    parts = lax.all_to_all(parts, "dp", 0, 0, axis_index_groups=ALONG_Y)
    results = adam(parts, basis, *(jnp.swapaxes(m, 0, 1) for m in (moment_one, moment_two)))
    return (feature_grad, *(jnp.swapaxes(r, 0, 1) for r in results))


def solution(mesh):
    in_specs = (
        P("dp", "tensor"),
        P("dp", "tensor"),
        P("dp", "tensor"),
        P(),
        P("tensor", "dp", None),
        P("tensor", "dp", None),
    )
    out_specs = (
        P("dp", "tensor"),
        P("tensor", "dp", None),
        P("tensor", "dp", None),
        P("tensor", "dp", None),
    )
    return jax.shard_map(body, mesh=mesh, in_specs=in_specs, out_specs=out_specs, check_vma=False)
```

```python
import jax
import jax.numpy as jnp
from jax import lax
from jax.experimental import pallas as pl
from jax.experimental.pallas import tpu as pltpu
from jax.sharding import PartitionSpec as P

beta_one = 0.9
beta_two = 0.95
bias_one = 1.0 - 0.9**20
bias_two = 1.0 - 0.95**20
adam_epsilon = 1e-08

NX, NY, NC, NZ = 4, 8, 2, 8


def dp_of(x, y, c):
    return (x * NY + y) * NC + c


def here():
    dp = lax.axis_index("dp")
    y = lax.rem(lax.div(dp, NC), NY)
    return lax.div(dp, NY * NC), y, lax.rem(dp, NC), lax.axis_index("tensor")


CHIPS = [(x, y, c) for x in range(NX) for y in range(NY) for c in range(NC)]
ALONG_X = [[dp_of(x, y, c) for x in range(NX)] for y in range(NY) for c in range(NC)]
Y_ORDER = [0, 4, 1, 5, 2, 6, 3, 7]
ALONG_Y = [[dp_of(x, y, c) for y in Y_ORDER] for x in range(NX) for c in range(NC)]
SAME_PARITY = [
    [dp_of(x, p + 2 * j, c) for j in range(NY // 2)]
    for x in range(NX)
    for p in range(2)
    for c in range(NC)
]
TO_NEIGHBOUR = [(dp_of(x, y, c), dp_of(x, (y + 1 - 2 * c) % NY, c)) for x, y, c in CHIPS]
OTHER_CORE = [(dp_of(x, y, c), dp_of(x, y, 1 - c)) for x, y, c in CHIPS]

HOME = [
    (dp_of(x, y, c) * NZ + 2 * q + h, dp_of((x + q) % NX, y, c) * NZ + 2 * x + h)
    for x, y, c in CHIPS
    for q in range(NX)
    for h in range(2)
]

FINISH_FLOPS = int(4e9)
FIRST_FLOPS = int(1e9)
SECOND_FLOPS = int(1e9)
NEAR_FLOPS = int(1e9)
NEAR_VMEM = 24_000_000
Z_ORDER = [0, 4, 1, 5, 2, 6, 3, 7]
ALONG_Z = [Z_ORDER]

VMEM_BYTES = 24 * 1024 * 1024
FIRST_VMEM = 53_000_000
SECOND_VMEM = 53_000_000


def whole(count):
    return [pl.BlockSpec(memory_space=pltpu.VMEM)] * count


def in_hbm(count):
    return [pl.BlockSpec(memory_space=pltpu.HBM)] * count


def spread_kernel(grads, out_ref, sems):
    copies = [pltpu.make_async_copy(grads, out_ref.at[x], sems.at[x]) for x in range(NX)]
    for copy in copies:
        copy.start()
    for copy in copies:
        copy.wait()


def spread(grads):
    return pl.pallas_call(
        spread_kernel,
        out_shape=jax.ShapeDtypeStruct((NX,) + grads.shape, grads.dtype),
        in_specs=whole(1),
        out_specs=in_hbm(1)[0],
        scratch_shapes=[pltpu.SemaphoreType.DMA((NX,))],
    )(grads)


FOLD = 4


def folded(block):
    step = block.shape[0] // FOLD
    return jnp.concatenate([block[k * step : (k + 1) * step] for k in range(FOLD)], axis=1)


def unfolded(block):
    step = block.shape[1] // FOLD
    return jnp.concatenate([block[:, k * step : (k + 1) * step] for k in range(FOLD)], axis=0)


def times(left, rows):
    return lax.dot_general(
        left[...], rows, (((1,), (1,)), ((), ())), preferred_element_type=jnp.float32
    ).astype(jnp.bfloat16)


def other_rows(same_other, k):
    height = same_other.shape[0] // (NY // 2)
    return jnp.concatenate(
        [same_other[(2 * h + k) * height : (2 * h + k + 1) * height, :] for h in range(2)], axis=0
    )


def fill(buffer, at, tokens, product):
    width = product.shape[1] // 2
    for block in range(NX):
        for h in range(2):
            part = product[block * tokens : (block + 1) * tokens, h * width : (h + 1) * width]
            if at is None:
                buffer[2 * block + h, tokens:, :] = folded(part)
            else:
                buffer[2 * block + h, :tokens, at : at + width] = part


def slot_of(q, h):
    slot = Z_ORDER.index(h)
    for k in range(1, NX):
        slot = jnp.where(q == k, Z_ORDER.index(2 * k + h), slot)
    return slot


def send(buffer, out_ref, x, sems):
    copies = []
    for block in range(NX):
        for h in range(2):
            k = 2 * block + h
            piece = slot_of(lax.rem(block - x + NX, NX), h)
            copies.append(pltpu.make_async_copy(buffer.at[k], out_ref.at[piece], sems.at[k]))
            copies[-1].start()
    for copy in copies:
        copy.wait()


def first_kernel(left, same, same_other, features, basis, out_ref, part, buffer, sems, sem):
    x, _, _, z = here()
    tokens, width = features.shape
    rank = basis.shape[1]
    start = pl.multiple_of(z * width, width)
    copy = pltpu.make_async_copy(basis.at[pl.ds(start, width), :], part, sem)
    copy.start()
    fill(buffer, 0, tokens, times(left, same[...]))
    fill(buffer, None, tokens, times(left, other_rows(same_other, 0)))
    copy.wait()
    coords = jnp.dot(features[...], part[...], preferred_element_type=jnp.float32).astype(
        jnp.bfloat16
    )
    for k in range(NZ):
        buffer[k, :tokens, buffer.shape[2] - rank :] = coords
    send(buffer, out_ref, x, sems)


def near_kernel(same, same_other, near_ref):
    _, _, core, _ = here()
    for k, rows in enumerate((same, same_other)):
        for j in range(NY // 4):
            near_ref[k, j] = rows[NY // 4 * core + j]


def rest_kernel(left, same_other, near, far, out_ref, right, buffer, sems):
    x, _, core, _ = here()
    height = near.shape[2]
    tokens = left.shape[0] // NX

    def place(j, c, rows):
        at = pl.multiple_of((NC * j + c) * height, height)
        right[pl.ds(at, height), :] = rows

    for j in range(NY // 4):
        for source, half in ((near, core), (far, 1 - core)):
            place(NY // 4 * half + j, half, source[0, j])
            place(NY // 4 * half + j, 1 - half, source[1, j])
    fill(buffer, None, tokens, times(left, other_rows(same_other, 1)))
    fill(buffer, 0, tokens, times(left, right[...]))
    send(buffer, out_ref, x, sems)


def flat(rows):
    return rows.reshape(-1, rows.shape[-1])


def first_tiles(grads, same, same_other, features, basis):
    tokens, width = features.shape
    rank = basis.shape[1]
    same, same_other = flat(same), flat(same_other)
    shape = (NZ, tokens + tokens // FOLD, same.shape[0] // 2 + rank)
    return pl.pallas_call(
        first_kernel,
        out_shape=jax.ShapeDtypeStruct(shape, jnp.bfloat16),
        in_specs=whole(4) + in_hbm(1),
        out_specs=in_hbm(1)[0],
        scratch_shapes=[
            pltpu.VMEM((width, rank), jnp.bfloat16),
            pltpu.VMEM(shape, jnp.bfloat16),
            pltpu.SemaphoreType.DMA((NZ,)),
            pltpu.SemaphoreType.DMA,
        ],
        compiler_params=pltpu.CompilerParams(vmem_limit_bytes=FIRST_VMEM),
        cost_estimate=pl.CostEstimate(flops=FIRST_FLOPS, bytes_accessed=0, transcendentals=0),
    )(flat(grads), same, same_other, features, basis)


def neighbour_rows(same, same_other):
    count, height, hidden = same.shape
    return pl.pallas_call(
        near_kernel,
        out_shape=jax.ShapeDtypeStruct((2, count // 2, height, hidden), jnp.bfloat16),
        in_specs=whole(2),
        out_specs=whole(1)[0],
        compiler_params=pltpu.CompilerParams(vmem_limit_bytes=NEAR_VMEM),
        cost_estimate=pl.CostEstimate(flops=NEAR_FLOPS, bytes_accessed=0, transcendentals=0),
    )(same, same_other)


def rest_tiles(grads, same_other, near, far):
    tokens, hidden = grads.shape[1:]
    same_other = flat(same_other)
    rows = (near.size + far.size) // hidden
    shape = (NZ, tokens + tokens // FOLD, rows // 2)
    return pl.pallas_call(
        rest_kernel,
        out_shape=jax.ShapeDtypeStruct(shape, jnp.bfloat16),
        in_specs=whole(4),
        out_specs=in_hbm(1)[0],
        scratch_shapes=[
            pltpu.VMEM((rows, hidden), jnp.bfloat16),
            pltpu.VMEM(shape, jnp.bfloat16),
            pltpu.SemaphoreType.DMA((NZ,)),
        ],
        compiler_params=pltpu.CompilerParams(vmem_limit_bytes=SECOND_VMEM),
        cost_estimate=pl.CostEstimate(flops=SECOND_FLOPS, bytes_accessed=0, transcendentals=0),
    )(flat(grads), same_other, near, far)


def sum_kernel(pieces, summed_ref, coords_ref):
    total = jnp.sum(pieces[...].astype(jnp.float32), axis=0)
    tokens, rank = coords_ref.shape
    width = total.shape[1] - rank
    summed_ref[:, :width] = total[:tokens, :width]
    summed_ref[:, width:] = unfolded(total[tokens:])
    coords_ref[...] = total[:tokens, width:].astype(jnp.bfloat16)


def sum_first(pieces, rank):
    tokens = pieces.shape[1] * FOLD // (FOLD + 1)
    width = pieces.shape[2]
    return pl.pallas_call(
        sum_kernel,
        out_shape=(
            jax.ShapeDtypeStruct((tokens, width - rank + width // FOLD), jnp.float32),
            jax.ShapeDtypeStruct((tokens, rank), jnp.bfloat16),
        ),
        in_specs=whole(1),
        out_specs=tuple(whole(2)),
        compiler_params=pltpu.CompilerParams(vmem_limit_bytes=VMEM_BYTES),
    )(pieces)


def join_kernel(first, pieces, out_ref):
    total = jnp.sum(pieces[...].astype(jnp.float32), axis=0)
    tokens, width = first.shape
    out_ref[:, :width] = first[...].astype(jnp.bfloat16)
    rest = unfolded(total[tokens:])
    out_ref[:, width : width + rest.shape[1]] = rest.astype(jnp.bfloat16)
    out_ref[:, width + rest.shape[1] :] = total[:tokens].astype(jnp.bfloat16)


def join(first, pieces):
    tokens, width = first.shape
    columns = width + pieces.shape[2] // FOLD + pieces.shape[2]
    return pl.pallas_call(
        join_kernel,
        out_shape=jax.ShapeDtypeStruct((tokens, columns), jnp.bfloat16),
        in_specs=whole(2),
        out_specs=whole(1)[0],
        compiler_params=pltpu.CompilerParams(vmem_limit_bytes=VMEM_BYTES),
    )(first, pieces)


def finish_kernel(parts, out_ref):
    _, y, core, _ = here()
    parity = lax.rem(y, 2)
    width = out_ref.shape[1] // (NY // 2 * NC)
    for k in range(2):
        mine = parts[:, k * width : (k + 1) * width]
        other = parts[:, (2 + k) * width : (3 + k) * width]
        for odd in range(2):
            for c in range(NC):
                crossed = parts[:, (4 + NC * k + c) * width : (5 + NC * k + c) * width]
                at = ((2 * k + odd) * NC + c) * width
                out_ref[:, at : at + width] = jnp.where(
                    parity == odd, jnp.where(core == c, mine, other), crossed
                )


def finish(parts):
    return pl.pallas_call(
        finish_kernel,
        out_shape=jax.ShapeDtypeStruct(parts.shape, jnp.bfloat16),
        in_specs=whole(1),
        out_specs=pl.BlockSpec(memory_space=pltpu.VMEM),
        compiler_params=pltpu.CompilerParams(vmem_limit_bytes=VMEM_BYTES),
        cost_estimate=pl.CostEstimate(flops=FINISH_FLOPS, bytes_accessed=0, transcendentals=0),
    )(parts)


def proj_kernel(grads, coords, mine_ref, other_ref, proj):
    proj[...] = lax.dot_general(
        grads[...], coords[...], (((0,), (0,)), ((), ())), preferred_element_type=jnp.float32
    )
    x, _, core, _ = here()
    parts, share, _ = mine_ref.shape
    rows = parts * NC * share
    own = proj[pl.ds(pl.multiple_of(x * rows, rows), rows), :]
    first_core = core == 0
    for k in range(parts):
        at = NC * k * share
        zero, one = own[at : at + share], own[at + share : at + NC * share]
        mine_ref[Y_ORDER.index(k)] = jnp.where(first_core, zero, one)
        other_ref[Y_ORDER.index(k)] = jnp.where(first_core, one, zero)


def project(grads, coords):
    hidden, rank = grads.shape[2], coords.shape[1]
    part = jax.ShapeDtypeStruct((NY, hidden // (NX * NY * NC), rank), jnp.float32)
    return pl.pallas_call(
        proj_kernel,
        out_shape=(part, part),
        in_specs=whole(2),
        out_specs=tuple(whole(2)),
        scratch_shapes=[pltpu.VMEM((hidden, rank), jnp.float32)],
        compiler_params=pltpu.CompilerParams(vmem_limit_bytes=VMEM_BYTES),
    )(grads.reshape(-1, hidden), coords)


def adam_kernel(parts_ref, basis_ref, one_ref, two_ref, new_one_ref, new_two_ref, direction_ref):
    projected = jnp.sum(parts_ref[...], axis=0)
    new_one = beta_one * one_ref[:, 0, :] + (1.0 - beta_one) * projected
    new_two = beta_two * two_ref[:, 0, :] + (1.0 - beta_two) * projected * projected
    new_one_ref[:, 0, :] = new_one
    new_two_ref[:, 0, :] = new_two
    step_dir = new_one / bias_one / (jnp.sqrt(new_two / bias_two) + adam_epsilon)
    direction_ref[:, 0, :] = lax.dot_general(
        step_dir.astype(jnp.bfloat16),
        basis_ref[...],
        (((1,), (1,)), ((), ())),
        preferred_element_type=jnp.float32,
    )


def adam(parts, basis, one, two):
    rows = one.shape[0]
    return pl.pallas_call(
        adam_kernel,
        out_shape=(
            jax.ShapeDtypeStruct(one.shape, jnp.float32),
            jax.ShapeDtypeStruct(one.shape, jnp.float32),
            jax.ShapeDtypeStruct((rows, 1, basis.shape[0]), jnp.float32),
        ),
        in_specs=whole(4),
        out_specs=tuple(whole(3)),
        compiler_params=pltpu.CompilerParams(vmem_limit_bytes=VMEM_BYTES),
    )(parts, basis, one, two)


def body(features, out_grad, weight, basis, moment_one, moment_two):
    grads = lax.all_to_all(spread(out_grad), "dp", 0, 0, axis_index_groups=ALONG_X)
    same = lax.all_gather(weight, "dp", axis=0, axis_index_groups=SAME_PARITY)

    same_other = lax.ppermute(same, "dp", OTHER_CORE)
    first = first_tiles(grads, same, same_other, features, basis)
    first, same, same_other = lax.optimization_barrier((first, same, same_other))
    first = lax.all_to_all(first, "tensor", 0, 0, axis_index_groups=ALONG_Z)

    near = lax.ppermute(neighbour_rows(same, same_other), "dp", TO_NEIGHBOUR)
    far = lax.ppermute(near, "dp", OTHER_CORE)
    second = rest_tiles(grads, same_other, near, far)
    first, second = lax.optimization_barrier((first, second))
    second = lax.all_to_all(second, "tensor", 0, 0, axis_index_groups=ALONG_Z)
    first, coords = sum_first(first, basis.shape[1])

    coords = lax.all_gather(coords, "dp", axis=0, tiled=True, axis_index_groups=ALONG_X)
    parts, other = project(grads, coords)
    parts = parts + lax.ppermute(other, "dp", OTHER_CORE)
    parts, second = lax.optimization_barrier((parts, second))

    summed = lax.ppermute(join(first, second), ("dp", "tensor"), HOME)
    feature_grad = finish(summed)

    parts = lax.all_to_all(parts, "dp", 0, 0, axis_index_groups=ALONG_Y)
    results = adam(parts, basis, *(jnp.swapaxes(m, 0, 1) for m in (moment_one, moment_two)))
    return (feature_grad, *(jnp.swapaxes(r, 0, 1) for r in results))


def solution(mesh):
    in_specs = (
        P("dp", "tensor"),
        P("dp", "tensor"),
        P("dp", "tensor"),
        P(),
        P("tensor", "dp", None),
        P("tensor", "dp", None),
    )
    out_specs = (
        P("dp", "tensor"),
        P("tensor", "dp", None),
        P("tensor", "dp", None),
        P("tensor", "dp", None),
    )
    return jax.shard_map(body, mesh=mesh, in_specs=in_specs, out_specs=out_specs, check_vma=False)
```

```python
import jax
import jax.numpy as jnp
from jax import lax
from jax.experimental import pallas as pl
from jax.experimental.pallas import tpu as pltpu
from jax.sharding import PartitionSpec as P

beta_one = 0.9
beta_two = 0.95
bias_one = 1.0 - 0.9**20
bias_two = 1.0 - 0.95**20
adam_epsilon = 1e-08

NX, NY, NC, NZ = 4, 8, 2, 8


def dp_of(x, y, c):
    return (x * NY + y) * NC + c


def here():
    dp = lax.axis_index("dp")
    y = lax.rem(lax.div(dp, NC), NY)
    return lax.div(dp, NY * NC), y, lax.rem(dp, NC), lax.axis_index("tensor")


CHIPS = [(x, y, c) for x in range(NX) for y in range(NY) for c in range(NC)]
ALONG_X = [[dp_of(x, y, c) for x in range(NX)] for y in range(NY) for c in range(NC)]
Y_ORDER = [0, 4, 1, 5, 2, 6, 3, 7]
ALONG_Y = [[dp_of(x, y, c) for y in Y_ORDER] for x in range(NX) for c in range(NC)]
SAME_PARITY = [
    [dp_of(x, p + 2 * j, c) for j in range(NY // 2)]
    for x in range(NX)
    for p in range(2)
    for c in range(NC)
]
TO_NEIGHBOUR = [(dp_of(x, y, c), dp_of(x, (y + 1 - 2 * c) % NY, c)) for x, y, c in CHIPS]
OTHER_CORE = [(dp_of(x, y, c), dp_of(x, y, 1 - c)) for x, y, c in CHIPS]

HOME = [
    (dp_of(x, y, c) * NZ + 2 * q + h, dp_of((x + q) % NX, y, c) * NZ + 2 * x + h)
    for x, y, c in CHIPS
    for q in range(NX)
    for h in range(2)
]

FINISH_FLOPS = int(4e9)
FIRST_FLOPS = int(1e9)
SECOND_FLOPS = int(1e9)
Z_ORDER = [0, 4, 1, 5, 2, 6, 3, 7]
ALONG_Z = [Z_ORDER]

VMEM_BYTES = 24 * 1024 * 1024
FIRST_VMEM = 53_000_000
SECOND_VMEM = 53_000_000


def whole(count):
    return [pl.BlockSpec(memory_space=pltpu.VMEM)] * count


def in_hbm(count):
    return [pl.BlockSpec(memory_space=pltpu.HBM)] * count


def spread_kernel(grads, out_ref, sems):
    copies = [pltpu.make_async_copy(grads, out_ref.at[x], sems.at[x]) for x in range(NX)]
    for copy in copies:
        copy.start()
    for copy in copies:
        copy.wait()


def spread(grads):
    return pl.pallas_call(
        spread_kernel,
        out_shape=jax.ShapeDtypeStruct((NX,) + grads.shape, grads.dtype),
        in_specs=whole(1),
        out_specs=in_hbm(1)[0],
        scratch_shapes=[pltpu.SemaphoreType.DMA((NX,))],
    )(grads)


FOLD = 4


def folded(block):
    step = block.shape[0] // FOLD
    return jnp.concatenate([block[k * step : (k + 1) * step] for k in range(FOLD)], axis=1)


def unfolded(block):
    step = block.shape[1] // FOLD
    return jnp.concatenate([block[:, k * step : (k + 1) * step] for k in range(FOLD)], axis=0)


def times(left, rows):
    return lax.dot_general(
        left[...], rows, (((1,), (1,)), ((), ())), preferred_element_type=jnp.float32
    ).astype(jnp.bfloat16)


def other_rows(same_other, k):
    height = same_other.shape[0] // (NY // 2)
    return jnp.concatenate(
        [same_other[(2 * h + k) * height : (2 * h + k + 1) * height, :] for h in range(2)], axis=0
    )


def fill(buffer, at, tokens, product):
    width = product.shape[1] // 2
    for block in range(NX):
        for h in range(2):
            part = product[block * tokens : (block + 1) * tokens, h * width : (h + 1) * width]
            if at is None:
                buffer[2 * block + h, tokens:, :] = folded(part)
            else:
                buffer[2 * block + h, :tokens, at : at + width] = part


def slot_of(q, h):
    slot = Z_ORDER.index(h)
    for k in range(1, NX):
        slot = jnp.where(q == k, Z_ORDER.index(2 * k + h), slot)
    return slot


def send(buffer, out_ref, x, sems):
    copies = []
    for block in range(NX):
        for h in range(2):
            k = 2 * block + h
            piece = slot_of(lax.rem(block - x + NX, NX), h)
            copies.append(pltpu.make_async_copy(buffer.at[k], out_ref.at[piece], sems.at[k]))
            copies[-1].start()
    for copy in copies:
        copy.wait()


def first_kernel(
    left, same, same_other, features, basis, out_ref, near_ref, part, buffer, sems, near_sems, sem
):
    x, _, core, z = here()
    _, count, height, _ = near_ref.shape
    nears = []
    for k, rows in enumerate((same, same_other)):
        for j in range(count):
            at = pl.multiple_of((count * core + j) * height, height)
            nears.append(
                pltpu.make_async_copy(
                    rows.at[pl.ds(at, height)], near_ref.at[k, j], near_sems.at[k, j]
                )
            )
            nears[-1].start()
    tokens, width = features.shape
    rank = basis.shape[1]
    start = pl.multiple_of(z * width, width)
    copy = pltpu.make_async_copy(basis.at[pl.ds(start, width), :], part, sem)
    copy.start()
    fill(buffer, 0, tokens, times(left, same[...]))
    fill(buffer, None, tokens, times(left, other_rows(same_other, 0)))
    copy.wait()
    coords = jnp.dot(features[...], part[...], preferred_element_type=jnp.float32).astype(
        jnp.bfloat16
    )
    for k in range(NZ):
        buffer[k, :tokens, buffer.shape[2] - rank :] = coords
    send(buffer, out_ref, x, sems)
    for near in nears:
        near.wait()


def rest_kernel(left, same_other, near, far, out_ref, right, buffer, sems):
    x, _, core, _ = here()
    height = near.shape[2]
    tokens = left.shape[0] // NX

    def place(j, c, rows):
        at = pl.multiple_of((NC * j + c) * height, height)
        right[pl.ds(at, height), :] = rows

    for j in range(NY // 4):
        for source, half in ((near, core), (far, 1 - core)):
            place(NY // 4 * half + j, half, source[0, j])
            place(NY // 4 * half + j, 1 - half, source[1, j])
    fill(buffer, None, tokens, times(left, other_rows(same_other, 1)))
    fill(buffer, 0, tokens, times(left, right[...]))
    send(buffer, out_ref, x, sems)


def flat(rows):
    return rows.reshape(-1, rows.shape[-1])


def first_tiles(grads, same, same_other, features, basis):
    tokens, width = features.shape
    rank = basis.shape[1]
    count, height, hidden = same.shape
    same, same_other = flat(same), flat(same_other)
    shape = (NZ, tokens + tokens // FOLD, same.shape[0] // 2 + rank)
    return pl.pallas_call(
        first_kernel,
        out_shape=(
            jax.ShapeDtypeStruct(shape, jnp.bfloat16),
            jax.ShapeDtypeStruct((2, count // 2, height, hidden), jnp.bfloat16),
        ),
        in_specs=whole(4) + in_hbm(1),
        out_specs=tuple(in_hbm(2)),
        scratch_shapes=[
            pltpu.VMEM((width, rank), jnp.bfloat16),
            pltpu.VMEM(shape, jnp.bfloat16),
            pltpu.SemaphoreType.DMA((NZ,)),
            pltpu.SemaphoreType.DMA((2, count // 2)),
            pltpu.SemaphoreType.DMA,
        ],
        compiler_params=pltpu.CompilerParams(vmem_limit_bytes=FIRST_VMEM),
        cost_estimate=pl.CostEstimate(flops=FIRST_FLOPS, bytes_accessed=0, transcendentals=0),
    )(flat(grads), same, same_other, features, basis)


def rest_tiles(grads, same_other, near, far):
    tokens, hidden = grads.shape[1:]
    same_other = flat(same_other)
    rows = (near.size + far.size) // hidden
    shape = (NZ, tokens + tokens // FOLD, rows // 2)
    return pl.pallas_call(
        rest_kernel,
        out_shape=jax.ShapeDtypeStruct(shape, jnp.bfloat16),
        in_specs=whole(4),
        out_specs=in_hbm(1)[0],
        scratch_shapes=[
            pltpu.VMEM((rows, hidden), jnp.bfloat16),
            pltpu.VMEM(shape, jnp.bfloat16),
            pltpu.SemaphoreType.DMA((NZ,)),
        ],
        compiler_params=pltpu.CompilerParams(vmem_limit_bytes=SECOND_VMEM),
        cost_estimate=pl.CostEstimate(flops=SECOND_FLOPS, bytes_accessed=0, transcendentals=0),
    )(flat(grads), same_other, near, far)


def sum_kernel(pieces, summed_ref, coords_ref):
    total = jnp.sum(pieces[...].astype(jnp.float32), axis=0)
    tokens, rank = coords_ref.shape
    width = total.shape[1] - rank
    summed_ref[:, :width] = total[:tokens, :width]
    summed_ref[:, width:] = unfolded(total[tokens:])
    coords_ref[...] = total[:tokens, width:].astype(jnp.bfloat16)


def sum_first(pieces, rank):
    tokens = pieces.shape[1] * FOLD // (FOLD + 1)
    width = pieces.shape[2]
    return pl.pallas_call(
        sum_kernel,
        out_shape=(
            jax.ShapeDtypeStruct((tokens, width - rank + width // FOLD), jnp.float32),
            jax.ShapeDtypeStruct((tokens, rank), jnp.bfloat16),
        ),
        in_specs=whole(1),
        out_specs=tuple(whole(2)),
        compiler_params=pltpu.CompilerParams(vmem_limit_bytes=VMEM_BYTES),
    )(pieces)


def join_kernel(first, pieces, out_ref):
    total = jnp.sum(pieces[...].astype(jnp.float32), axis=0)
    tokens, width = first.shape
    out_ref[:, :width] = first[...].astype(jnp.bfloat16)
    rest = unfolded(total[tokens:])
    out_ref[:, width : width + rest.shape[1]] = rest.astype(jnp.bfloat16)
    out_ref[:, width + rest.shape[1] :] = total[:tokens].astype(jnp.bfloat16)


def join(first, pieces):
    tokens, width = first.shape
    columns = width + pieces.shape[2] // FOLD + pieces.shape[2]
    return pl.pallas_call(
        join_kernel,
        out_shape=jax.ShapeDtypeStruct((tokens, columns), jnp.bfloat16),
        in_specs=whole(2),
        out_specs=whole(1)[0],
        compiler_params=pltpu.CompilerParams(vmem_limit_bytes=VMEM_BYTES),
    )(first, pieces)


def finish_kernel(parts, out_ref):
    _, y, core, _ = here()
    parity = lax.rem(y, 2)
    width = out_ref.shape[1] // (NY // 2 * NC)
    for k in range(2):
        mine = parts[:, k * width : (k + 1) * width]
        other = parts[:, (2 + k) * width : (3 + k) * width]
        for odd in range(2):
            for c in range(NC):
                crossed = parts[:, (4 + NC * k + c) * width : (5 + NC * k + c) * width]
                at = ((2 * k + odd) * NC + c) * width
                out_ref[:, at : at + width] = jnp.where(
                    parity == odd, jnp.where(core == c, mine, other), crossed
                )


def finish(parts):
    return pl.pallas_call(
        finish_kernel,
        out_shape=jax.ShapeDtypeStruct(parts.shape, jnp.bfloat16),
        in_specs=whole(1),
        out_specs=pl.BlockSpec(memory_space=pltpu.VMEM),
        compiler_params=pltpu.CompilerParams(vmem_limit_bytes=VMEM_BYTES),
        cost_estimate=pl.CostEstimate(flops=FINISH_FLOPS, bytes_accessed=0, transcendentals=0),
    )(parts)


def proj_kernel(grads, coords, mine_ref, other_ref, proj):
    proj[...] = lax.dot_general(
        grads[...], coords[...], (((0,), (0,)), ((), ())), preferred_element_type=jnp.float32
    )
    x, _, core, _ = here()
    parts, share, _ = mine_ref.shape
    rows = parts * NC * share
    own = proj[pl.ds(pl.multiple_of(x * rows, rows), rows), :]
    first_core = core == 0
    for k in range(parts):
        at = NC * k * share
        zero, one = own[at : at + share], own[at + share : at + NC * share]
        mine_ref[Y_ORDER.index(k)] = jnp.where(first_core, zero, one)
        other_ref[Y_ORDER.index(k)] = jnp.where(first_core, one, zero)


def project(grads, coords):
    hidden, rank = grads.shape[2], coords.shape[1]
    part = jax.ShapeDtypeStruct((NY, hidden // (NX * NY * NC), rank), jnp.float32)
    return pl.pallas_call(
        proj_kernel,
        out_shape=(part, part),
        in_specs=whole(2),
        out_specs=tuple(whole(2)),
        scratch_shapes=[pltpu.VMEM((hidden, rank), jnp.float32)],
        compiler_params=pltpu.CompilerParams(vmem_limit_bytes=VMEM_BYTES),
    )(grads.reshape(-1, hidden), coords)


def adam_kernel(parts_ref, basis_ref, one_ref, two_ref, new_one_ref, new_two_ref, direction_ref):
    projected = jnp.sum(parts_ref[...], axis=0)
    new_one = beta_one * one_ref[:, 0, :] + (1.0 - beta_one) * projected
    new_two = beta_two * two_ref[:, 0, :] + (1.0 - beta_two) * projected * projected
    new_one_ref[:, 0, :] = new_one
    new_two_ref[:, 0, :] = new_two
    step_dir = new_one / bias_one / (jnp.sqrt(new_two / bias_two) + adam_epsilon)
    direction_ref[:, 0, :] = lax.dot_general(
        step_dir.astype(jnp.bfloat16),
        basis_ref[...],
        (((1,), (1,)), ((), ())),
        preferred_element_type=jnp.float32,
    )


def adam(parts, basis, one, two):
    rows = one.shape[0]
    return pl.pallas_call(
        adam_kernel,
        out_shape=(
            jax.ShapeDtypeStruct(one.shape, jnp.float32),
            jax.ShapeDtypeStruct(one.shape, jnp.float32),
            jax.ShapeDtypeStruct((rows, 1, basis.shape[0]), jnp.float32),
        ),
        in_specs=whole(4),
        out_specs=tuple(whole(3)),
        compiler_params=pltpu.CompilerParams(vmem_limit_bytes=VMEM_BYTES),
    )(parts, basis, one, two)


def body(features, out_grad, weight, basis, moment_one, moment_two):
    grads = lax.all_to_all(spread(out_grad), "dp", 0, 0, axis_index_groups=ALONG_X)
    same = lax.all_gather(weight, "dp", axis=0, axis_index_groups=SAME_PARITY)

    same_other = lax.ppermute(same, "dp", OTHER_CORE)
    first, near = first_tiles(grads, same, same_other, features, basis)
    first = lax.all_to_all(first, "tensor", 0, 0, axis_index_groups=ALONG_Z)

    near = lax.ppermute(near, "dp", TO_NEIGHBOUR)
    far = lax.ppermute(near, "dp", OTHER_CORE)
    second = rest_tiles(grads, same_other, near, far)
    first, second = lax.optimization_barrier((first, second))
    second = lax.all_to_all(second, "tensor", 0, 0, axis_index_groups=ALONG_Z)
    first, coords = sum_first(first, basis.shape[1])

    coords = lax.all_gather(coords, "dp", axis=0, tiled=True, axis_index_groups=ALONG_X)
    parts, other = project(grads, coords)
    parts = parts + lax.ppermute(other, "dp", OTHER_CORE)
    parts, second = lax.optimization_barrier((parts, second))

    summed = lax.ppermute(join(first, second), ("dp", "tensor"), HOME)
    feature_grad = finish(summed)

    parts = lax.all_to_all(parts, "dp", 0, 0, axis_index_groups=ALONG_Y)
    results = adam(parts, basis, *(jnp.swapaxes(m, 0, 1) for m in (moment_one, moment_two)))
    return (feature_grad, *(jnp.swapaxes(r, 0, 1) for r in results))


def solution(mesh):
    in_specs = (
        P("dp", "tensor"),
        P("dp", "tensor"),
        P("dp", "tensor"),
        P(),
        P("tensor", "dp", None),
        P("tensor", "dp", None),
    )
    out_specs = (
        P("dp", "tensor"),
        P("tensor", "dp", None),
        P("tensor", "dp", None),
        P("tensor", "dp", None),
    )
    return jax.shard_map(body, mesh=mesh, in_specs=in_specs, out_specs=out_specs, check_vma=False)
```

```python
import jax
import jax.numpy as jnp
from jax import lax
from jax.experimental import pallas as pl
from jax.experimental.pallas import tpu as pltpu
from jax.sharding import PartitionSpec as P

beta_one = 0.9
beta_two = 0.95
bias_one = 1.0 - 0.9**20
bias_two = 1.0 - 0.95**20
adam_epsilon = 1e-08

NX, NY, NC, NZ = 4, 8, 2, 8


def dp_of(x, y, c):
    return (x * NY + y) * NC + c


def here():
    dp = lax.axis_index("dp")
    y = lax.rem(lax.div(dp, NC), NY)
    return lax.div(dp, NY * NC), y, lax.rem(dp, NC), lax.axis_index("tensor")


CHIPS = [(x, y, c) for x in range(NX) for y in range(NY) for c in range(NC)]
ALONG_X = [[dp_of(x, y, c) for x in range(NX)] for y in range(NY) for c in range(NC)]
Y_ORDER = [0, 4, 1, 5, 2, 6, 3, 7]
ALONG_Y = [[dp_of(x, y, c) for y in Y_ORDER] for x in range(NX) for c in range(NC)]
SAME_PARITY = [
    [dp_of(x, p + 2 * j, c) for j in range(NY // 2)]
    for x in range(NX)
    for p in range(2)
    for c in range(NC)
]
TO_NEIGHBOUR = [(dp_of(x, y, c), dp_of(x, (y + 1 - 2 * c) % NY, c)) for x, y, c in CHIPS]
OTHER_CORE = [(dp_of(x, y, c), dp_of(x, y, 1 - c)) for x, y, c in CHIPS]

HOME = [
    (dp_of(x, y, c) * NZ + 2 * q + h, dp_of((x + q) % NX, y, c) * NZ + 2 * x + h)
    for x, y, c in CHIPS
    for q in range(NX)
    for h in range(2)
]

FINISH_FLOPS = int(4e9)
FIRST_FLOPS = int(1e9)
SECOND_FLOPS = int(1e9)
Z_ORDER = [0, 4, 1, 5, 2, 6, 3, 7]
ALONG_Z = [Z_ORDER]

VMEM_BYTES = 24 * 1024 * 1024
FIRST_VMEM = 53_600_000
SECOND_VMEM = 53_000_000


def whole(count):
    return [pl.BlockSpec(memory_space=pltpu.VMEM)] * count


def in_hbm(count):
    return [pl.BlockSpec(memory_space=pltpu.HBM)] * count


def spread_kernel(grads, out_ref, sems):
    copies = [pltpu.make_async_copy(grads, out_ref.at[x], sems.at[x]) for x in range(NX)]
    for copy in copies:
        copy.start()
    for copy in copies:
        copy.wait()


def spread(grads):
    return pl.pallas_call(
        spread_kernel,
        out_shape=jax.ShapeDtypeStruct((NX,) + grads.shape, grads.dtype),
        in_specs=whole(1),
        out_specs=in_hbm(1)[0],
        scratch_shapes=[pltpu.SemaphoreType.DMA((NX,))],
    )(grads)


EARLY = 32


def folded(block, width):
    step = block.shape[0] * block.shape[1] // width
    return jnp.concatenate(
        [block[k * step : (k + 1) * step] for k in range(block.shape[0] // step)], axis=1
    )


def unfolded(block, columns):
    return jnp.concatenate(
        [block[:, k : k + columns] for k in range(0, block.shape[1], columns)], axis=0
    )


def times(left, rows):
    return lax.dot_general(
        left[...], rows, (((1,), (1,)), ((), ())), preferred_element_type=jnp.float32
    ).astype(jnp.bfloat16)


def other_rows(same_other, start, stop):
    half = same_other.shape[0] // 2
    return jnp.concatenate(
        [same_other[h * half + start : h * half + stop, :] for h in range(2)], axis=0
    )


def fill(buffer, tokens, product):
    width = product.shape[1] // 2
    for block in range(NX):
        for h in range(2):
            buffer[2 * block + h, :tokens, :width] = product[
                block * tokens : (block + 1) * tokens, h * width : (h + 1) * width
            ]


def fill_below(buffer, tokens, product):
    width = product.shape[1] // 2
    columns = buffer.shape[2]
    for block in range(NX):
        for h in range(2):
            part = product[block * tokens : (block + 1) * tokens, h * width : (h + 1) * width]
            at = tokens
            for start, stop in ((0, EARLY), (EARLY, width)):
                if start < stop:
                    below = folded(part[:, start:stop], columns)
                    buffer[2 * block + h, at : at + below.shape[0], :] = below
                    at += below.shape[0]


def slot_of(q, h):
    slot = Z_ORDER.index(h)
    for k in range(1, NX):
        slot = jnp.where(q == k, Z_ORDER.index(2 * k + h), slot)
    return slot


def send(buffer, out_ref, x, sems):
    copies = []
    for block in range(NX):
        for h in range(2):
            k = 2 * block + h
            piece = slot_of(lax.rem(block - x + NX, NX), h)
            copies.append(pltpu.make_async_copy(buffer.at[k], out_ref.at[piece], sems.at[k]))
            copies[-1].start()
    for copy in copies:
        copy.wait()


def first_kernel(
    left, same, same_other, features, basis, out_ref, near_ref, part, buffer, sems, near_sems, sem
):
    x, _, core, z = here()
    _, count, height, _ = near_ref.shape
    nears = []
    for k, rows in enumerate((same, same_other)):
        for j in range(count):
            at = pl.multiple_of((count * core + j) * height, height)
            nears.append(
                pltpu.make_async_copy(
                    rows.at[pl.ds(at, height)], near_ref.at[k, j], near_sems.at[k, j]
                )
            )
            nears[-1].start()
    tokens, width = features.shape
    rank = basis.shape[1]
    start = pl.multiple_of(z * width, width)
    copy = pltpu.make_async_copy(basis.at[pl.ds(start, width), :], part, sem)
    copy.start()
    fill(buffer, tokens, times(left, same[...]))
    fill_below(buffer, tokens, times(left, other_rows(same_other, 0, EARLY)))
    copy.wait()
    coords = jnp.dot(features[...], part[...], preferred_element_type=jnp.float32).astype(
        jnp.bfloat16
    )
    for k in range(NZ):
        buffer[k, :tokens, buffer.shape[2] - rank :] = coords
    send(buffer, out_ref, x, sems)
    for near in nears:
        near.wait()


def rest_kernel(left, same_other, near, far, out_ref, right, buffer, sems):
    x, _, core, _ = here()
    height = near.shape[2]
    tokens = left.shape[0] // NX

    def place(j, c, rows):
        at = pl.multiple_of((NC * j + c) * height, height)
        right[pl.ds(at, height), :] = rows

    for j in range(NY // 4):
        for source, half in ((near, core), (far, 1 - core)):
            place(NY // 4 * half + j, half, source[0, j])
            place(NY // 4 * half + j, 1 - half, source[1, j])
    fill_below(buffer, tokens, times(left, other_rows(same_other, EARLY, same_other.shape[0] // 2)))
    fill(buffer, tokens, times(left, right[...]))
    send(buffer, out_ref, x, sems)


def flat(rows):
    return rows.reshape(-1, rows.shape[-1])


def first_tiles(grads, same, same_other, features, basis):
    tokens, width = features.shape
    rank = basis.shape[1]
    count, height, hidden = same.shape
    same, same_other = flat(same), flat(same_other)
    columns = same.shape[0] // 2 + rank
    shape = (NZ, tokens + tokens * EARLY // columns, columns)
    return pl.pallas_call(
        first_kernel,
        out_shape=(
            jax.ShapeDtypeStruct(shape, jnp.bfloat16),
            jax.ShapeDtypeStruct((2, count // 2, height, hidden), jnp.bfloat16),
        ),
        in_specs=whole(4) + in_hbm(1),
        out_specs=tuple(in_hbm(2)),
        scratch_shapes=[
            pltpu.VMEM((width, rank), jnp.bfloat16),
            pltpu.VMEM(shape, jnp.bfloat16),
            pltpu.SemaphoreType.DMA((NZ,)),
            pltpu.SemaphoreType.DMA((2, count // 2)),
            pltpu.SemaphoreType.DMA,
        ],
        compiler_params=pltpu.CompilerParams(vmem_limit_bytes=FIRST_VMEM),
        cost_estimate=pl.CostEstimate(flops=FIRST_FLOPS, bytes_accessed=0, transcendentals=0),
    )(flat(grads), same, same_other, features, basis)


def rest_tiles(grads, same_other, near, far):
    tokens, hidden = grads.shape[1:]
    same_other = flat(same_other)
    rows = (near.size + far.size) // hidden
    late = same_other.shape[0] // 2 - EARLY
    shape = (NZ, tokens + tokens * late // (rows // 2), rows // 2)
    return pl.pallas_call(
        rest_kernel,
        out_shape=jax.ShapeDtypeStruct(shape, jnp.bfloat16),
        in_specs=whole(4),
        out_specs=in_hbm(1)[0],
        scratch_shapes=[
            pltpu.VMEM((rows, hidden), jnp.bfloat16),
            pltpu.VMEM(shape, jnp.bfloat16),
            pltpu.SemaphoreType.DMA((NZ,)),
        ],
        compiler_params=pltpu.CompilerParams(vmem_limit_bytes=SECOND_VMEM),
        cost_estimate=pl.CostEstimate(flops=SECOND_FLOPS, bytes_accessed=0, transcendentals=0),
    )(flat(grads), same_other, near, far)


def sum_kernel(pieces, summed_ref, coords_ref):
    total = jnp.sum(pieces[...].astype(jnp.float32), axis=0)
    tokens, rank = coords_ref.shape
    width = total.shape[1] - rank
    summed_ref[:, :width] = total[:tokens, :width]
    summed_ref[:, width:] = unfolded(total[tokens:], EARLY)
    coords_ref[...] = total[:tokens, width:].astype(jnp.bfloat16)


def sum_first(pieces, tokens, rank):
    width = pieces.shape[2]
    return pl.pallas_call(
        sum_kernel,
        out_shape=(
            jax.ShapeDtypeStruct((tokens, width - rank + EARLY), jnp.float32),
            jax.ShapeDtypeStruct((tokens, rank), jnp.bfloat16),
        ),
        in_specs=whole(1),
        out_specs=tuple(whole(2)),
        compiler_params=pltpu.CompilerParams(vmem_limit_bytes=VMEM_BYTES),
    )(pieces)


def join_kernel(first, pieces, out_ref):
    total = jnp.sum(pieces[...].astype(jnp.float32), axis=0)
    tokens, width = first.shape
    out_ref[:, :width] = first[...].astype(jnp.bfloat16)
    columns = total.shape[1]
    below = tokens
    late = (total.shape[0] - tokens) * columns // tokens
    for count in [c for c in (EARLY, late - EARLY) if c > 0]:
        rows = tokens * count // columns
        part = unfolded(total[below : below + rows], count)
        out_ref[:, width : width + count] = part.astype(jnp.bfloat16)
        below += rows
        width += count
    out_ref[:, width:] = total[:tokens].astype(jnp.bfloat16)


def join(first, pieces):
    tokens, width = first.shape
    columns = width + pieces.shape[1] * pieces.shape[2] // tokens
    return pl.pallas_call(
        join_kernel,
        out_shape=jax.ShapeDtypeStruct((tokens, columns), jnp.bfloat16),
        in_specs=whole(2),
        out_specs=whole(1)[0],
        compiler_params=pltpu.CompilerParams(vmem_limit_bytes=VMEM_BYTES),
    )(first, pieces)


def finish_kernel(parts, out_ref):
    _, y, core, _ = here()
    parity = lax.rem(y, 2)
    width = out_ref.shape[1] // (NY // 2 * NC)
    for k in range(2):
        mine = parts[:, k * width : (k + 1) * width]
        other = parts[:, (2 + k) * width : (3 + k) * width]
        for odd in range(2):
            for c in range(NC):
                crossed = parts[:, (4 + NC * k + c) * width : (5 + NC * k + c) * width]
                at = ((2 * k + odd) * NC + c) * width
                out_ref[:, at : at + width] = jnp.where(
                    parity == odd, jnp.where(core == c, mine, other), crossed
                )


def finish(parts):
    return pl.pallas_call(
        finish_kernel,
        out_shape=jax.ShapeDtypeStruct(parts.shape, jnp.bfloat16),
        in_specs=whole(1),
        out_specs=pl.BlockSpec(memory_space=pltpu.VMEM),
        compiler_params=pltpu.CompilerParams(vmem_limit_bytes=VMEM_BYTES),
        cost_estimate=pl.CostEstimate(flops=FINISH_FLOPS, bytes_accessed=0, transcendentals=0),
    )(parts)


def proj_kernel(grads, coords, mine_ref, other_ref, proj):
    proj[...] = lax.dot_general(
        grads[...], coords[...], (((0,), (0,)), ((), ())), preferred_element_type=jnp.float32
    )
    x, _, core, _ = here()
    parts, share, _ = mine_ref.shape
    rows = parts * NC * share
    own = proj[pl.ds(pl.multiple_of(x * rows, rows), rows), :]
    first_core = core == 0
    for k in range(parts):
        at = NC * k * share
        zero, one = own[at : at + share], own[at + share : at + NC * share]
        mine_ref[Y_ORDER.index(k)] = jnp.where(first_core, zero, one)
        other_ref[Y_ORDER.index(k)] = jnp.where(first_core, one, zero)


def project(grads, coords):
    hidden, rank = grads.shape[2], coords.shape[1]
    part = jax.ShapeDtypeStruct((NY, hidden // (NX * NY * NC), rank), jnp.float32)
    return pl.pallas_call(
        proj_kernel,
        out_shape=(part, part),
        in_specs=whole(2),
        out_specs=tuple(whole(2)),
        scratch_shapes=[pltpu.VMEM((hidden, rank), jnp.float32)],
        compiler_params=pltpu.CompilerParams(vmem_limit_bytes=VMEM_BYTES),
    )(grads.reshape(-1, hidden), coords)


def adam_kernel(parts_ref, basis_ref, one_ref, two_ref, new_one_ref, new_two_ref, direction_ref):
    projected = jnp.sum(parts_ref[...], axis=0)
    new_one = beta_one * one_ref[:, 0, :] + (1.0 - beta_one) * projected
    new_two = beta_two * two_ref[:, 0, :] + (1.0 - beta_two) * projected * projected
    new_one_ref[:, 0, :] = new_one
    new_two_ref[:, 0, :] = new_two
    step_dir = new_one / bias_one / (jnp.sqrt(new_two / bias_two) + adam_epsilon)
    direction_ref[:, 0, :] = lax.dot_general(
        step_dir.astype(jnp.bfloat16),
        basis_ref[...],
        (((1,), (1,)), ((), ())),
        preferred_element_type=jnp.float32,
    )


def adam(parts, basis, one, two):
    rows = one.shape[0]
    return pl.pallas_call(
        adam_kernel,
        out_shape=(
            jax.ShapeDtypeStruct(one.shape, jnp.float32),
            jax.ShapeDtypeStruct(one.shape, jnp.float32),
            jax.ShapeDtypeStruct((rows, 1, basis.shape[0]), jnp.float32),
        ),
        in_specs=whole(4),
        out_specs=tuple(whole(3)),
        compiler_params=pltpu.CompilerParams(vmem_limit_bytes=VMEM_BYTES),
    )(parts, basis, one, two)


def body(features, out_grad, weight, basis, moment_one, moment_two):
    grads = lax.all_to_all(spread(out_grad), "dp", 0, 0, axis_index_groups=ALONG_X)
    same = lax.all_gather(weight, "dp", axis=0, axis_index_groups=SAME_PARITY)

    same_other = lax.ppermute(same, "dp", OTHER_CORE)
    first, near = first_tiles(grads, same, same_other, features, basis)
    first = lax.all_to_all(first, "tensor", 0, 0, axis_index_groups=ALONG_Z)

    near = lax.ppermute(near, "dp", TO_NEIGHBOUR)
    far = lax.ppermute(near, "dp", OTHER_CORE)
    second = rest_tiles(grads, same_other, near, far)
    first, second = lax.optimization_barrier((first, second))
    second = lax.all_to_all(second, "tensor", 0, 0, axis_index_groups=ALONG_Z)
    first, coords = sum_first(first, features.shape[0], basis.shape[1])

    coords = lax.all_gather(coords, "dp", axis=0, tiled=True, axis_index_groups=ALONG_X)
    parts, other = project(grads, coords)
    parts = parts + lax.ppermute(other, "dp", OTHER_CORE)
    parts, second = lax.optimization_barrier((parts, second))

    summed = lax.ppermute(join(first, second), ("dp", "tensor"), HOME)
    feature_grad = finish(summed)

    parts = lax.all_to_all(parts, "dp", 0, 0, axis_index_groups=ALONG_Y)
    results = adam(parts, basis, *(jnp.swapaxes(m, 0, 1) for m in (moment_one, moment_two)))
    return (feature_grad, *(jnp.swapaxes(r, 0, 1) for r in results))


def solution(mesh):
    in_specs = (
        P("dp", "tensor"),
        P("dp", "tensor"),
        P("dp", "tensor"),
        P(),
        P("tensor", "dp", None),
        P("tensor", "dp", None),
    )
    out_specs = (
        P("dp", "tensor"),
        P("tensor", "dp", None),
        P("tensor", "dp", None),
        P("tensor", "dp", None),
    )
    return jax.shard_map(body, mesh=mesh, in_specs=in_specs, out_specs=out_specs, check_vma=False)
```
